128 devices in a mesh: seg: 4 (over y_lo, core), item: 8 (over x, y_hi), slot: 4 (over z).
Axes of the slice: x: 4, y: 4 (y_hi: 2, y_lo: 2; y = y_hi * 2 + y_lo), z: 4, core: 2. Of those that a mesh axis runs over, the one named last changes fastest.
Arguments:
- tensor: float32 [128, 2048, 2048], P('slot', 'seg', 'item'), may hold values from -200 to 200
- b_factor: float32 [2048, 512], P('item'), may hold values from -25 to 25
- c_factor: float32 [128, 512], P('slot'), may hold values from -25 to 25
Outputs:
- a_factor: float32 [2048, 512], P('seg')
- b_new: float32 [2048, 512], P('item')
- lambda_a: float32 [512], replicated
- lambda_b: float32 [512], replicated
The draws below stay inside these ranges and needn't reach their ends.
All inputs are finite; a program needn't handle non-finite values.
Results may differ from the reference program's by a relative error of at most 0.00027.
Values sent between devices are 32-bit elements; how exact they have to be, the bound alone decides.
No kernel may reach another device: no remote copies, remote signals or barrier semaphores. Data moves between devices by JAX's collectives and lax.ppermute only.
A program may use at most 128 MiB of HBM per device.

```python
import jax
import jax.numpy as jnp
from jax import lax

RANK = 512
SEGMENTS = 2048
ITEMS = 2048
SLOTS = 128


SHARED_WEIGHT = 0.3162


SHARED_COUNT = 16


def draw_tensor(key, part):
    key = jax.random.fold_in(key, 7)
    key_base, key_rows, key_cols = jax.random.split(key, 3)
    row_ramp = 10.0 ** (jnp.arange(SEGMENTS, dtype=jnp.float32) / max(SEGMENTS - 1, 1))
    row_scale = row_ramp * jax.random.uniform(key_rows, (SEGMENTS,), jnp.float32, 0.8, 1.25)
    col_ramp = 10.0 ** (jnp.arange(ITEMS, dtype=jnp.float32) / max(ITEMS - 1, 1) - 0.5)
    col_scale = col_ramp * jax.random.uniform(key_cols, (ITEMS,), jnp.float32, 0.8, 1.25)
    base_values = jnp.clip(jax.random.normal(key_base, (SLOTS, SEGMENTS, ITEMS), jnp.float32), -4.0, 4.0)
    return (base_values * row_scale[None, :, None] * col_scale[None, None, :]).astype(jnp.float32)


def shared_part(key, row_count, weight_low):
    key_left, key_right = jax.random.split(key, 2)
    left_values = jnp.clip(jax.random.normal(key_left, (row_count, SHARED_COUNT), jnp.float32), -4.0, 4.0)
    right_values = jax.random.uniform(key_right, (SHARED_COUNT, RANK), jnp.float32, weight_low, 1.0)
    total = jnp.zeros((row_count, RANK), jnp.float32)
    for index in range(SHARED_COUNT):
        total = total + left_values[:, index:index + 1] * right_values[index:index + 1, :]
    return total


def draw_b_factor(key, part):
    key = jax.random.fold_in(key, 11)
    key_noise, key_shared = jax.random.split(key, 2)
    noise = jnp.clip(jax.random.normal(key_noise, (ITEMS, RANK), jnp.float32), -4.0, 4.0)
    common = shared_part(key_shared, ITEMS, 0.0)
    return ((noise + SHARED_WEIGHT * common) * float(ITEMS) ** (-0.5)).astype(jnp.float32)


def draw_c_factor(key, part):
    key = jax.random.fold_in(key, 13)
    key_noise, key_shared = jax.random.split(key, 2)
    noise = jnp.clip(jax.random.normal(key_noise, (SLOTS, RANK), jnp.float32), -4.0, 4.0)
    common = shared_part(key_shared, SLOTS, 0.0)
    return ((noise + SHARED_WEIGHT * common) * float(SLOTS) ** (-0.5)).astype(jnp.float32)


def setup_inputs(seed: int = 0) -> dict:
    keys = jax.random.split(jax.random.key(seed), 4)
    tensor = draw_tensor(jax.random.fold_in(keys[3], 71), 0)
    b_factor = draw_b_factor(jax.random.fold_in(keys[3], 71), 0)
    c_factor = draw_c_factor(jax.random.fold_in(keys[3], 71), 0)
    return dict(tensor=tensor, b_factor=b_factor, c_factor=c_factor)


RIDGE_WEIGHT = 0.1
EPSILON = 1e-06
HIGHEST = lax.Precision.HIGHEST

def gram_of(row_block):
    return lax.dot_general(row_block.astype(jnp.float32), row_block.astype(jnp.float32), (((0,), (0,)), ((), ())), precision=HIGHEST, preferred_element_type=jnp.float32)

def solve_rows(right_side, system):
    lower_factor = jnp.linalg.cholesky(system)
    half_solved = lax.linalg.triangular_solve(lower_factor, right_side, left_side=False, lower=True, transpose_a=True)
    return lax.linalg.triangular_solve(lower_factor, half_solved, left_side=False, lower=True, transpose_a=False)

def reference(tensor, b_factor, c_factor):
    identity_matrix = jnp.eye(RANK, dtype=jnp.float32)
    gram_b = gram_of(b_factor)
    gram_c = gram_of(c_factor)

    def step_one(carry, pieces):
        slab, weights = pieces
        scaled = b_factor * weights[None, :]
        return (carry + jnp.dot(slab.astype(jnp.float32), scaled.astype(jnp.float32), precision=HIGHEST, preferred_element_type=jnp.float32), None)
    mode_one, unused = lax.scan(step_one, jnp.zeros((SEGMENTS, RANK), jnp.float32), (tensor, c_factor))
    segment_raw = solve_rows(mode_one, gram_b * gram_c + RIDGE_WEIGHT * identity_matrix)
    lambda_a = jnp.sqrt(lax.optimization_barrier(jnp.sum(segment_raw * segment_raw, axis=0)) / SEGMENTS + EPSILON)
    a_factor = segment_raw / lambda_a[None, :]
    gram_a = gram_of(a_factor)

    def step_two(carry, pieces):
        slab, weights = pieces
        scaled = a_factor * weights[None, :]
        term = lax.dot_general(slab.astype(jnp.float32), scaled.astype(jnp.float32), (((0,), (0,)), ((), ())), precision=HIGHEST, preferred_element_type=jnp.float32)
        return (carry + term, None)
    mode_two, unused = lax.scan(step_two, jnp.zeros((ITEMS, RANK), jnp.float32), (tensor, c_factor))
    item_raw = solve_rows(mode_two, gram_a * gram_c + RIDGE_WEIGHT * identity_matrix)
    lambda_b = jnp.sqrt(lax.optimization_barrier(jnp.sum(item_raw * item_raw, axis=0)) / ITEMS + EPSILON)
    b_new = item_raw / lambda_b[None, :]
    return (a_factor, b_new, lambda_a, lambda_b)
```

```python
import functools

import jax
import jax.numpy as jnp
from jax import lax
from jax.experimental import pallas as pl
from jax.experimental.pallas import tpu as pltpu
from jax.sharding import PartitionSpec as P

RIDGE_WEIGHT = 0.1
EPSILON = 1e-06
HIGHEST = lax.Precision.HIGHEST
BLOCK = 128
PANEL = 16
STEP = 8
VMEM = pl.BlockSpec(memory_space=pltpu.VMEM)
PARAMS = pltpu.CompilerParams(vmem_limit_bytes=48 * 1024 * 1024)


def dot_full(left, right, left_dim=1):
    return lax.dot_general(
        left, right, (((left_dim,), (0,)), ((), ())), precision=HIGHEST, preferred_element_type=jnp.float32
    )


def split_two(values):
    high = values.astype(jnp.bfloat16)
    return high, (values - high.astype(jnp.float32)).astype(jnp.bfloat16)


def strip_place(strip):
    return ((0, 0), (1, 0), (1, 3 * BLOCK), (0, 4 * BLOCK))[strip]


def store_gram(rows, strips_ref):
    width = rows.shape[1]
    for strip in range(width // BLOCK):
        slab, start = strip_place(strip)
        low = strip * BLOCK
        strips_ref[slab, :, start:start + width - low] = dot_full(rows[:, low:low + BLOCK], rows[:, low:], 0)


def gram_kernel(rows_ref, strips_ref):
    store_gram(rows_ref[...], strips_ref)


def strips_shape(width):
    return jax.ShapeDtypeStruct((2, BLOCK, width + BLOCK), jnp.float32)


def gram_strips(rows):
    return pl.pallas_call(
        gram_kernel,
        out_shape=strips_shape(rows.shape[1]),
        in_specs=[VMEM],
        out_specs=VMEM,
        compiler_params=PARAMS,
    )(rows)


def contraction_kernel(slab_ref, factor_ref, weight_ref, start_ref, out_ref, parts_ref, *, contract, fresh):
    depth = factor_ref.shape[0]

    @pl.when(pl.program_id(0) == 0)
    def _():
        high, low = split_two(factor_ref[...])
        parts_ref[0:depth, :] = high
        parts_ref[depth:2 * depth, :] = high
        parts_ref[2 * depth:3 * depth, :] = low
        out_ref[...] = jnp.zeros_like(out_ref) if fresh else start_ref[...]

    for k in range(STEP):
        high, low = split_two(slab_ref[k])
        pieces = jnp.concatenate([high, low, high], axis=contract)
        term = lax.dot_general(
            pieces, parts_ref[...], (((contract,), (0,)), ((), ())), preferred_element_type=jnp.float32
        )
        out_ref[...] += term * weight_ref[0, k:k + 1, :]


def contraction(tensor, factor, weights, contract, first, last, start=None):
    slots, rows, cols = tensor.shape
    depth, width = factor.shape
    out_rows = rows if contract == 1 else cols
    fresh = start is None
    if fresh:
        start = jnp.zeros((8, 128), jnp.float32)
    count = last - first
    weights = weights.reshape(slots // STEP, STEP, width)
    return pl.pallas_call(
        functools.partial(contraction_kernel, contract=contract, fresh=fresh),
        grid=(count,),
        in_specs=[
            pl.BlockSpec((STEP, rows, cols), lambda g: (g + first, 0, 0)),
            pl.BlockSpec((depth, width), lambda g: (0, 0)),
            pl.BlockSpec((1, STEP, width), lambda g: (g + first, 0, 0)),
            pl.BlockSpec(start.shape, lambda g: (0, 0)),
        ],
        out_specs=pl.BlockSpec((out_rows, width), lambda g: (0, 0)),
        out_shape=jax.ShapeDtypeStruct((out_rows, width), jnp.float32),
        scratch_shapes=[pltpu.VMEM((3 * depth, width), jnp.bfloat16)],
        compiler_params=PARAMS,
        cost_estimate=pl.CostEstimate(
            flops=9 * count * STEP * rows * cols * width,
            bytes_accessed=count * STEP * rows * cols * 4,
            transcendentals=0,
        ),
    )(tensor, factor, weights, start)


def invert_block(block):
    size = block.shape[0]
    shape = (PANEL, size)
    sub = lax.broadcasted_iota(jnp.int32, shape, 0)
    lane = lax.broadcasted_iota(jnp.int32, shape, 1)
    row_index = lax.broadcasted_iota(jnp.int32, (size, size), 0)
    col_index = lax.broadcasted_iota(jnp.int32, (size, size), 1)
    for low in range(0, size, PANEL):
        high = low + PANEL
        panel = block[low:high, :]
        columns = [jnp.broadcast_to(panel[:, low + t:low + t + 1], shape) for t in range(PANEL)]
        result = jnp.where((lane >= low) & (lane < high), jnp.where(lane - low == sub, 1.0, 0.0), panel)
        for t in range(PANEL):
            here = sub == t
            column = columns[t]
            scale = 1.0 / column[t:t + 1, :]
            for u in range(t + 1, PANEL):
                pivot = columns[u][t:t + 1, :] * scale
                columns[u] = jnp.where(here, jnp.broadcast_to(pivot, shape), columns[u] - column * pivot)
            pivot = result[t:t + 1, :] * scale
            result = jnp.where(here, jnp.broadcast_to(pivot, shape), result - column * pivot)
        parts = [result]
        if low:
            parts.insert(0, jnp.zeros((low, size), jnp.float32))
        if high < size:
            parts.append(jnp.zeros((size - high, size), jnp.float32))
        padded = jnp.concatenate(parts, axis=0)
        update = dot_full(block, padded)
        kept = jnp.where((col_index >= low) & (col_index < high), 0.0, block)
        block = jnp.where((row_index >= low) & (row_index < high), padded, kept - update)
    return block


def eliminate(matrix_ref, first, last):
    size = matrix_ref.shape[0]

    def step(p, carry):
        low = pl.multiple_of(p * BLOCK, BLOCK)
        here = pl.ds(low, BLOCK)
        inverse = invert_block(matrix_ref[here, here])
        column = matrix_ref[:, here]
        matrix_ref[:, here] = jnp.zeros((size, BLOCK), jnp.float32)
        matrix_ref[here, here] = jnp.eye(BLOCK, dtype=jnp.float32)
        row = dot_full(inverse, matrix_ref[here, :])
        matrix_ref[...] = matrix_ref[...] - dot_full(column, row)
        matrix_ref[here, :] = row
        return carry

    lax.fori_loop(first, last, step, 0)


def first_half_kernel(strips_ref, slots_ref, matrix_ref, scale_ref, *, rows_total):
    size = matrix_ref.shape[0]
    blocks = size // BLOCK
    diagonal = lax.broadcasted_iota(jnp.int32, (BLOCK, BLOCK), 0) == lax.broadcasted_iota(
        jnp.int32, (BLOCK, BLOCK), 1
    )
    if rows_total is None:
        scale_ref[...] = jnp.ones_like(scale_ref)
    else:
        for p in range(blocks):
            slab, start = strip_place(p)
            squares = jnp.where(diagonal, strips_ref[slab, :, start:start + BLOCK], 0.0)
            scale_ref[:, p * BLOCK:(p + 1) * BLOCK] = jnp.sqrt(
                jnp.sum(squares, axis=0, keepdims=True) / rows_total + EPSILON
            )
    for p in range(blocks):
        slab, start = strip_place(p)
        low = p * BLOCK
        gram = strips_ref[slab, :, start:start + size - low]
        if rows_total is not None:
            squares = jnp.where(diagonal, gram[:, 0:BLOCK], 0.0)
            scale = jnp.sqrt(jnp.sum(squares, axis=1, keepdims=True) / rows_total + EPSILON)
            gram = gram / scale / scale_ref[:, low:]
        system = gram * dot_full(slots_ref[:, low:low + BLOCK], slots_ref[:, low:], 0)
        matrix_ref[low:low + BLOCK, low:] = system
        matrix_ref[low:low + BLOCK, low:low + BLOCK] = system[:, 0:BLOCK] + jnp.where(diagonal, RIDGE_WEIGHT, 0.0)
        for q in range(p + 1, blocks):
            matrix_ref[q * BLOCK:(q + 1) * BLOCK, low:low + BLOCK] = system[
                :, (q - p) * BLOCK:(q - p + 1) * BLOCK
            ].T
    eliminate(matrix_ref, 0, blocks // 2)


def first_half(strips, slots_all, rows_total):
    size = slots_all.shape[1]
    return pl.pallas_call(
        functools.partial(first_half_kernel, rows_total=rows_total),
        out_shape=(
            jax.ShapeDtypeStruct((size, size), jnp.float32),
            jax.ShapeDtypeStruct((1, size), jnp.float32),
        ),
        in_specs=[VMEM, VMEM],
        out_specs=(VMEM, VMEM),
        compiler_params=PARAMS,
        cost_estimate=pl.CostEstimate(flops=12 * 10**9, bytes_accessed=2**20, transcendentals=0),
    )(strips, slots_all)


def second_half_kernel(matrix_ref, out_ref):
    blocks = matrix_ref.shape[0] // BLOCK
    out_ref[...] = matrix_ref[...]
    eliminate(out_ref, blocks // 2, blocks)


def second_half(matrix):
    return pl.pallas_call(
        second_half_kernel,
        out_shape=jax.ShapeDtypeStruct(matrix.shape, jnp.float32),
        in_specs=[VMEM],
        out_specs=VMEM,
        compiler_params=PARAMS,
        cost_estimate=pl.CostEstimate(flops=12 * 10**9, bytes_accessed=2**20, transcendentals=0),
    )(matrix)


def solve_one_kernel(total_ref, inverse_ref, raw_ref, strips_ref):
    raw = dot_full(total_ref[...], inverse_ref[...])
    raw_ref[...] = raw
    store_gram(raw, strips_ref)


def solve_one(total, inverse):
    return pl.pallas_call(
        solve_one_kernel,
        out_shape=(jax.ShapeDtypeStruct(total.shape, jnp.float32), strips_shape(total.shape[1])),
        in_specs=[VMEM, VMEM],
        out_specs=(VMEM, VMEM),
        compiler_params=PARAMS,
    )(total, inverse)


def solve_two_kernel(total_ref, scale_ref, inverse_ref, raw_ref, squares_ref):
    raw = dot_full(total_ref[...] / scale_ref[...], inverse_ref[...])
    raw_ref[...] = raw
    squares_ref[...] = jnp.sum(raw * raw, axis=0, keepdims=True)


def solve_two(total, scale, inverse):
    return pl.pallas_call(
        solve_two_kernel,
        out_shape=(
            jax.ShapeDtypeStruct(total.shape, jnp.float32),
            jax.ShapeDtypeStruct((1, total.shape[1]), jnp.float32),
        ),
        in_specs=[VMEM, VMEM, VMEM],
        out_specs=(VMEM, VMEM),
        compiler_params=PARAMS,
    )(total, scale, inverse)


def exchange(values, axes):
    return lax.all_to_all(values, axes, 0, 0, tiled=True)


def scattered_sum(received, parts):
    rows, cols = received.shape
    return jnp.sum(received.reshape(parts, rows // parts, cols), axis=0)


def spread(values, axes, parts):
    rows, cols = values.shape
    copies = jnp.broadcast_to(values[None], (parts, rows, cols)).reshape(parts * rows, cols)
    return exchange(copies, axes)


def swap(values, axis, mask):
    return lax.ppermute(values, axis, [(i, i ^ mask) for i in range(lax.axis_size(axis))])


def local(tensor, b_factor, c_factor):
    width = b_factor.shape[1]
    segs, items, slots = (lax.axis_size(name) for name in ("seg", "item", "slot"))
    steps = tensor.shape[0] // STEP
    slab_rows = width + BLOCK

    slots_all = spread(c_factor, "slot", slots)
    b_strips = gram_strips(b_factor).reshape(2 * BLOCK, slab_rows)
    b_received = exchange(b_strips, "item")
    one = contraction(tensor, b_factor, c_factor, 1, 0, steps)
    b_received, one = lax.optimization_barrier((b_received, one))
    b_strips = spread(scattered_sum(b_received, items), "item", items).reshape(2, BLOCK, slab_rows)
    one_received = exchange(one, ("item", "slot"))

    matrix, unused = first_half(b_strips, slots_all, None)
    matrix, one_received = lax.optimization_barrier((matrix, one_received))
    one_total = spread(scattered_sum(one_received, items * slots), ("item", "slot"), items * slots)
    inverse = second_half(matrix)
    segment_raw, a_strips = solve_one(one_total, inverse)

    core = lax.axis_index("seg") % 2
    mine = lax.dynamic_index_in_dim(a_strips, core, 0, keepdims=False)
    other = lax.dynamic_index_in_dim(a_strips, 1 - core, 0, keepdims=False)
    arrived = swap(other, "seg", 1)
    two = contraction(tensor, segment_raw, c_factor, 0, 0, 1)
    arrived, two = lax.optimization_barrier((arrived, two))
    mine = mine + arrived
    arrived = swap(mine, "seg", 2)
    two = contraction(tensor, segment_raw, c_factor, 0, 1, 3, two)
    arrived, two = lax.optimization_barrier((arrived, two))
    mine = mine + arrived
    arrived = swap(mine, "seg", 1)
    two = contraction(tensor, segment_raw, c_factor, 0, 3, steps, two)
    a_strips = jnp.where(core == 0, jnp.stack([mine, arrived]), jnp.stack([arrived, mine]))

    two_received = exchange(two, ("seg", "slot"))
    matrix, scale = first_half(a_strips, slots_all, tensor.shape[1] * segs)
    matrix, two_received = lax.optimization_barrier((matrix, two_received))
    two_total = spread(scattered_sum(two_received, segs * slots), ("seg", "slot"), segs * slots)
    inverse = second_half(matrix)
    a_factor = segment_raw / scale
    item_raw, squares = solve_two(two_total, scale, inverse)
    squares = jnp.sum(spread(squares, "item", items), axis=0)
    lambda_b = jnp.sqrt(squares / (tensor.shape[2] * items) + EPSILON)
    b_new = item_raw / lambda_b[None, :]
    return (a_factor, b_new, scale.reshape(width), lambda_b)


def solution(mesh):
    placed = (P("slot", "seg", "item"), P("item", None), P("slot", None))
    return jax.shard_map(
        local,
        mesh=mesh,
        in_specs=placed,
        out_specs=(P("seg", None), P("item", None), P(), P()),
        check_vma=False,
    )
```

```python
import functools

import jax
import jax.numpy as jnp
from jax import lax
from jax.experimental import pallas as pl
from jax.experimental.pallas import tpu as pltpu
from jax.sharding import PartitionSpec as P

RIDGE_WEIGHT = 0.1
EPSILON = 1e-06
HIGHEST = lax.Precision.HIGHEST
BLOCK = 128
PANEL = 16
GROUP = 4
VMEM = pl.BlockSpec(memory_space=pltpu.VMEM)
HBM = pl.BlockSpec(memory_space=pltpu.HBM)
PARAMS = pltpu.CompilerParams(vmem_limit_bytes=24 * 1024 * 1024)


def dot_full(left, right, left_dim=1):
    return lax.dot_general(
        left, right, (((left_dim,), (0,)), ((), ())), precision=HIGHEST, preferred_element_type=jnp.float32
    )


def dot_parts(left, right):
    return lax.dot_general(left, right, (((1,), (0,)), ((), ())), preferred_element_type=jnp.float32)


def split_two(values):
    high = values.astype(jnp.bfloat16)
    return high, (values - high.astype(jnp.float32)).astype(jnp.bfloat16)


def strip_place(strip):
    return ((0, 0), (1, 0), (1, 3 * BLOCK), (0, 4 * BLOCK))[strip]


def core_index():
    return lax.rem(lax.axis_index("seg"), 2)


def store_gram(rows, strips_ref):
    width = rows.shape[1]
    core = core_index()
    for strip in range(width // BLOCK):
        slab, start = strip_place(strip)
        low = strip * BLOCK
        place = core if slab == 0 else 1 - core
        strips_ref[place, :, start:start + width - low] = dot_full(rows[:, low:low + BLOCK], rows[:, low:], 0)


def store_parts(values, parts_ref):
    depth = values.shape[0]
    high, low = split_two(values)
    parts_ref[0:depth, :] = high
    parts_ref[depth:2 * depth, :] = high
    parts_ref[2 * depth:3 * depth, :] = low


def gram_kernel(rows_ref, *refs):
    piece_refs, parts_ref, strips_ref = refs[:-2], refs[-2], refs[-1]
    rows = rows_ref[...]
    store_gram(rows, strips_ref)
    along = lax.axis_index("item") // 2
    height = piece_refs[0].shape[0]
    for ahead, ref in enumerate(piece_refs):
        owner = lax.rem(along + ahead, len(piece_refs))
        ref[...] = strips_ref[0, pl.ds(pl.multiple_of(owner * height, height), height), :]
    store_parts(rows, parts_ref)


def slab_shape(width):
    return (BLOCK, width + BLOCK)


def gram_pieces(rows, count):
    depth, width = rows.shape
    piece = jax.ShapeDtypeStruct((BLOCK // count, width + BLOCK), jnp.float32)
    return pl.pallas_call(
        gram_kernel,
        out_shape=(piece,) * count + (jax.ShapeDtypeStruct((3 * depth, width), jnp.bfloat16),),
        in_specs=[VMEM],
        out_specs=(VMEM,) * (count + 1),
        scratch_shapes=[pltpu.VMEM((2, *slab_shape(width)), jnp.float32)],
        compiler_params=PARAMS,
    )(rows)


def contraction_kernel(*refs, contract, first, last, ahead, load):
    if load:
        source_ref, parts_ref, weight_ref, *start_refs, out_ref, tensor_ref, pieces_ref, arrived = refs
    else:
        parts_ref, weight_ref, *start_refs, tensor_ref, out_ref, unused, pieces_ref = refs
    depth = parts_ref.shape[0] // 3
    cols = tensor_ref.shape[2]
    height = tensor_ref.shape[1]
    rows = pl.ds(0, height)
    if ahead is not None:
        slots = lax.axis_size("slot")
        height = height // slots

        def quarter(distance):
            return pl.ds(pl.multiple_of(lax.rem(lax.axis_index("slot") + distance, slots) * height, height), height)

        rows = quarter(ahead)
    group = GROUP if contract == 1 else 1
    half = pieces_ref.shape[0] // 2

    waiting = {}
    if load:
        total_slots = tensor_ref.shape[0]
        if ahead is None:
            bounds = (first, first + 1, first + 3, last, (last + total_slots) // 2, total_slots)
        else:
            bounds = (0, 4, 12, total_slots)
        steps = [(rows, low, high) for low, high in zip(bounds, bounds[1:])]
        if ahead is not None:
            steps += [(quarter(ahead + distance), 0, total_slots) for distance in range(1, slots)]
        for n, (place, low, high) in enumerate(steps):
            here = (pl.ds(low, high - low), place, slice(None))
            waiting[n] = pltpu.make_async_copy(source_ref.at[here], tensor_ref.at[here], arrived.at[n])
            waiting[n].start()

    def prepare(k):
        for n in list(waiting):
            if steps[n][0] is rows and steps[n][1] == k:
                waiting.pop(n).wait()
        here = pl.ds(k // group % 2 * half, half)
        upper, lower = split_two(tensor_ref[k:k + group, rows, :].reshape(group * height, cols))
        pieces_ref[here, 0:depth] = upper if contract == 1 else upper.T
        pieces_ref[here, depth:2 * depth] = lower if contract == 1 else lower.T

    def product(k):
        here = pl.ds(k // group % 2 * half, half)
        return dot_parts(pieces_ref[here, :], parts_ref[0:2 * depth, :]) + dot_parts(
            pieces_ref[here, 0:depth], parts_ref[2 * depth:3 * depth, :]
        )

    size = half // group
    prepare(first)
    for k in range(first, last, group):
        if k + group < last:
            prepare(k + group)
        term = product(k)
        total = sum(term[n * size:(n + 1) * size, :] * weight_ref[k + n:k + n + 1, :] for n in range(group))
        if k == first:
            out_ref[0:size, :] = sum((ref[0:size, :] for ref in start_refs), total)
        else:
            out_ref[0:size, :] += total
    if out_ref.shape[0] > size:
        out_ref[size:, :] = weight_ref[...]
    for copy in waiting.values():
        copy.wait()


def contraction(tensor, parts, weights, contract, first, last, start=(), ahead=None, load=False):
    slots, rows, cols = tensor.shape
    width = parts.shape[1]
    height = rows if ahead is None else rows // lax.axis_size("slot")
    out_rows = height if contract == 1 else cols
    if ahead:
        out_rows += slots
    count = last - first
    kernel = functools.partial(contraction_kernel, contract=contract, first=first, last=last, ahead=ahead, load=load)
    inputs = [parts, weights, *start]
    out_shape = jax.ShapeDtypeStruct((out_rows, width), jnp.float32)
    pieces = pltpu.VMEM((2 * (GROUP * height if contract == 1 else cols), 2 * parts.shape[0] // 3), jnp.bfloat16)
    return pl.pallas_call(
        kernel,
        in_specs=[HBM] + [VMEM] * len(inputs) if load else [VMEM] * (len(inputs) + 1),
        out_specs=(VMEM, VMEM),
        out_shape=(out_shape, jax.ShapeDtypeStruct(tensor.shape, tensor.dtype)),
        scratch_shapes=[pieces] + ([pltpu.SemaphoreType.DMA((6,))] if load else []),
        input_output_aliases={} if load else {len(inputs): 1},
        compiler_params=PARAMS,
        cost_estimate=pl.CostEstimate(
            flops=9 * count * height * cols * width,
            bytes_accessed=count * height * cols * 4,
            transcendentals=0,
        ),
    )(*([tensor] + inputs if load else inputs + [tensor]))


def finish_one_kernel(own_ref, slots_ref, *refs):
    *arrived_refs, total_ref, slots_all_ref = refs
    height, depth = own_ref.shape[0], slots_ref.shape[0]
    total_ref[...] = own_ref[...] + arrived_refs[-1][0:height, :]
    slots_all_ref[0:depth, :] = slots_ref[...]
    for n, ref in enumerate(arrived_refs):
        slots_all_ref[(n + 1) * depth:(n + 2) * depth, :] = ref[height:, :]


def finish_one(own, slots, arrived):
    return pl.pallas_call(
        finish_one_kernel,
        out_shape=(
            jax.ShapeDtypeStruct(own.shape, jnp.float32),
            jax.ShapeDtypeStruct((slots.shape[0] * (1 + len(arrived)), slots.shape[1]), jnp.float32),
        ),
        in_specs=[VMEM] * (2 + len(arrived)),
        out_specs=(VMEM, VMEM),
        compiler_params=PARAMS,
    )(own, slots, *arrived)


def invert_block(block):
    size = block.shape[0]
    shape = (PANEL, size)
    sub = lax.broadcasted_iota(jnp.int32, shape, 0)
    lane = lax.broadcasted_iota(jnp.int32, shape, 1)
    row_index = lax.broadcasted_iota(jnp.int32, (size, size), 0)
    col_index = lax.broadcasted_iota(jnp.int32, (size, size), 1)
    panel = block[0:PANEL, :]
    for low in range(0, size, PANEL):
        high = low + PANEL
        columns = [jnp.broadcast_to(panel[:, low + t:low + t + 1], shape) for t in range(PANEL)]
        result = jnp.where((lane >= low) & (lane < high), jnp.where(lane - low == sub, 1.0, 0.0), panel)
        for t in range(PANEL):
            here = sub == t
            column = columns[t]
            scale = 1.0 / column[t:t + 1, :]
            for u in range(t + 1, PANEL):
                pivot = columns[u][t:t + 1, :] * scale
                columns[u] = jnp.where(here, jnp.broadcast_to(pivot, shape), columns[u] - column * pivot)
            pivot = result[t:t + 1, :] * scale
            result = jnp.where(here, jnp.broadcast_to(pivot, shape), result - column * pivot)
        if high < size:
            ahead = block[high:high + PANEL, :]
            panel = jnp.where((lane >= low) & (lane < high), 0.0, ahead)
            sums = [None] * 4
            for t in range(PANEL):
                term = jnp.broadcast_to(ahead[:, low + t:low + t + 1], shape) * result[t:t + 1, :]
                sums[t % 4] = term if sums[t % 4] is None else sums[t % 4] + term
            panel = panel - ((sums[0] + sums[1]) + (sums[2] + sums[3]))
        parts = [result]
        if low:
            parts.insert(0, jnp.zeros((low, size), jnp.float32))
        if high < size:
            parts.append(jnp.zeros((size - high, size), jnp.float32))
        padded = jnp.concatenate(parts, axis=0)
        update = dot_full(block, padded)
        kept = jnp.where((col_index >= low) & (col_index < high), 0.0, block)
        block = jnp.where((row_index >= low) & (row_index < high), padded, kept - update)
    return block


def eliminate(matrix_ref, first, last):
    size = matrix_ref.shape[0]

    def step(p, carry):
        low = pl.multiple_of(p * BLOCK, BLOCK)
        here = pl.ds(low, BLOCK)
        inverse = invert_block(matrix_ref[here, here])
        column = matrix_ref[:, here]
        matrix_ref[:, here] = jnp.zeros((size, BLOCK), jnp.float32)
        matrix_ref[here, here] = jnp.eye(BLOCK, dtype=jnp.float32)
        row = dot_full(inverse, matrix_ref[here, :])
        matrix_ref[...] = matrix_ref[...] - dot_full(column, row)
        matrix_ref[here, :] = row
        return carry

    lax.fori_loop(first, last, step, 0)


def place_rows(piece_refs, strips_ref):
    core = core_index()
    item = lax.axis_index("item")
    along = item // 2
    count, height, unused = piece_refs[0].shape
    for other_core, ref in enumerate(piece_refs):
        slab = core if other_core == 0 else 1 - core
        for back in range(count):
            owner = lax.rem(along + count - back, count)
            strips_ref[slab, pl.ds(pl.multiple_of(owner * height, height), height), :] = ref[back]


def place_slabs(piece_refs, strips_ref):
    core = core_index()
    strips_ref[core] = piece_refs[0][...]
    strips_ref[1 - core] = piece_refs[1][...]


def first_half_kernel(mine_ref, arrived_ref, slots_ref, matrix_ref, scale_ref, strips_ref, *, rows_total):
    size = matrix_ref.shape[0]
    blocks = size // BLOCK
    diagonal = lax.broadcasted_iota(jnp.int32, (BLOCK, BLOCK), 0) == lax.broadcasted_iota(
        jnp.int32, (BLOCK, BLOCK), 1
    )
    slots = slots_ref[...]
    if rows_total is None:
        place_rows((mine_ref, arrived_ref), strips_ref)
        scale_ref[...] = jnp.ones_like(scale_ref)
    else:
        place_slabs((mine_ref, arrived_ref), strips_ref)
        for p in range(blocks):
            slab, start = strip_place(p)
            squares = jnp.where(diagonal, strips_ref[slab, :, start:start + BLOCK], 0.0)
            scale_ref[:, p * BLOCK:(p + 1) * BLOCK] = jnp.sqrt(
                jnp.sum(squares, axis=0, keepdims=True) / rows_total + EPSILON
            )
    for p in range(blocks):
        slab, start = strip_place(p)
        low = p * BLOCK
        gram = strips_ref[slab, :, start:start + size - low]
        if rows_total is not None:
            squares = jnp.where(diagonal, gram[:, 0:BLOCK], 0.0)
            scale = jnp.sqrt(jnp.sum(squares, axis=1, keepdims=True) / rows_total + EPSILON)
            gram = gram / scale / scale_ref[:, low:]
        system = gram * dot_full(slots[:, low:low + BLOCK], slots[:, low:], 0)
        matrix_ref[low:low + BLOCK, low:] = system
        matrix_ref[low:low + BLOCK, low:low + BLOCK] = system[:, 0:BLOCK] + jnp.where(diagonal, RIDGE_WEIGHT, 0.0)
        for q in range(p + 1, blocks):
            matrix_ref[q * BLOCK:(q + 1) * BLOCK, low:low + BLOCK] = system[
                :, (q - p) * BLOCK:(q - p + 1) * BLOCK
            ].T
    eliminate(matrix_ref, 0, blocks // 2)


def first_half(mine, arrived, slots_all, rows_total):
    size = slots_all.shape[1]
    return pl.pallas_call(
        functools.partial(first_half_kernel, rows_total=rows_total),
        out_shape=(
            jax.ShapeDtypeStruct((size, size), jnp.float32),
            jax.ShapeDtypeStruct((1, size), jnp.float32),
        ),
        in_specs=[VMEM] * 3,
        out_specs=(VMEM, VMEM),
        scratch_shapes=[pltpu.VMEM((2, *slab_shape(size)), jnp.float32)],
        compiler_params=PARAMS,
        cost_estimate=pl.CostEstimate(flops=12 * 10**9, bytes_accessed=2**20, transcendentals=0),
    )(mine, arrived, slots_all)


def second_half_kernel(matrix_ref, after_ref, out_ref):
    blocks = matrix_ref.shape[0] // BLOCK
    out_ref[...] = matrix_ref[...]
    eliminate(out_ref, blocks // 2, blocks)


def second_half(matrix, after):
    return pl.pallas_call(
        second_half_kernel,
        out_shape=jax.ShapeDtypeStruct(matrix.shape, jnp.float32),
        in_specs=[VMEM, VMEM],
        out_specs=VMEM,
        input_output_aliases={0: 0},
        compiler_params=PARAMS,
        cost_estimate=pl.CostEstimate(flops=12 * 10**9, bytes_accessed=2**20, transcendentals=0),
    )(matrix, after)


def solve_one_kernel(total_ref, inverse_ref, raw_ref, parts_ref, mine_ref, other_ref, strips_ref, *, items, slots):
    height = total_ref.shape[0] // (items * slots)
    count = items * slots
    blocks = [total_ref[n * height:(n + 1) * height, :] for z in range(slots) for n in range(z, count, slots)]
    raw = dot_full(jnp.concatenate(blocks, axis=0), inverse_ref[...])
    raw_ref[...] = raw
    store_gram(raw, strips_ref)
    mine_ref[...] = strips_ref[0]
    other_ref[...] = strips_ref[1]
    store_parts(raw, parts_ref)


def solve_one(total, inverse, items, slots):
    depth, width = total.shape
    slab = jax.ShapeDtypeStruct(slab_shape(width), jnp.float32)
    return pl.pallas_call(
        functools.partial(solve_one_kernel, items=items, slots=slots),
        out_shape=(
            jax.ShapeDtypeStruct(total.shape, jnp.float32),
            jax.ShapeDtypeStruct((3 * depth, width), jnp.bfloat16),
            slab,
            slab,
        ),
        in_specs=[VMEM, VMEM],
        out_specs=(VMEM,) * 4,
        scratch_shapes=[pltpu.VMEM((2, *slab_shape(width)), jnp.float32)],
        compiler_params=PARAMS,
    )(total, inverse)


def solve_two_kernel(total_ref, scale_ref, inverse_ref, raw_ref, squares_ref):
    raw = dot_full(total_ref[...] / scale_ref[...], inverse_ref[...])
    raw_ref[...] = raw
    squares_ref[...] = jnp.broadcast_to(jnp.sum(raw * raw, axis=0, keepdims=True), squares_ref.shape)


def solve_two(total, scale, inverse, copies):
    return pl.pallas_call(
        solve_two_kernel,
        out_shape=(
            jax.ShapeDtypeStruct(total.shape, jnp.float32),
            jax.ShapeDtypeStruct((copies, total.shape[1]), jnp.float32),
        ),
        in_specs=[VMEM, VMEM, VMEM],
        out_specs=(VMEM, VMEM),
        compiler_params=PARAMS,
    )(total, scale, inverse)


def exchange(values, axes):
    return lax.all_to_all(values, axes, 0, 0, tiled=True)


def sum_and_copy_kernel(received_ref, copies_ref, *, parts):
    height = received_ref.shape[0] // parts
    total = received_ref[0:height, :]
    for p in range(1, parts):
        total = total + received_ref[p * height:(p + 1) * height, :]
    for p in range(copies_ref.shape[0] // height):
        copies_ref[p * height:(p + 1) * height, :] = total


def sum_and_spread(received, parts, axes, copies):
    rows, cols = received.shape
    copied = pl.pallas_call(
        functools.partial(sum_and_copy_kernel, parts=parts),
        out_shape=jax.ShapeDtypeStruct((rows // parts * copies, cols), jnp.float32),
        in_specs=[VMEM],
        out_specs=VMEM,
        compiler_params=PARAMS,
    )(received)
    return exchange(copied, axes)


def swap(values, axis, mask):
    return lax.ppermute(values, axis, [(i, i ^ mask) for i in range(lax.axis_size(axis))])


def shift(values, axis, table):
    return lax.ppermute(values, axis, list(enumerate(table)))


def local(tensor, b_factor, c_factor):
    width = b_factor.shape[1]
    segs, items, slots = (lax.axis_size(name) for name in ("seg", "item", "slot"))
    depth = tensor.shape[0]

    def to_slot(value, d):
        return shift(value, "slot", [(i + d) % slots for i in range(slots)])

    def along_x(value, d):
        return shift(value, "item", [(i + 2 * d) % items for i in range(items)])

    *b_pieces, b_parts = gram_pieces(b_factor, items // 2)

    def part_one(held, ahead, start=(), load=False):
        return contraction(held, b_parts, c_factor, 1, 0, depth, start, ahead, load)

    arrived = [along_x(b_pieces[d], d) for d in range(1, items // 2)]
    two_ahead, held = part_one(tensor, 2, load=True)
    *arrived, two_ahead = lax.optimization_barrier((*arrived, two_ahead))
    piece = sum(arrived, b_pieces[0])
    other = swap(piece, "item", 1)
    two_ahead = to_slot(two_ahead, 2)
    one_ahead, held = part_one(held, 1)
    other, one_ahead = lax.optimization_barrier((other, one_ahead))
    piece = piece + other
    one_ahead = to_slot(one_ahead, 1)
    pieces = [piece] + [along_x(piece, d) for d in range(1, items // 2)]
    three_ahead, held = part_one(held, 3)
    *pieces, three_ahead = lax.optimization_barrier((*pieces, three_ahead))
    three_ahead = to_slot(three_ahead, 3)
    pieces = jnp.stack(pieces)
    arrived = swap(pieces, "seg", 1)
    own, held = part_one(held, 0, (two_ahead, one_ahead))
    arrived, own, three_ahead = lax.optimization_barrier((arrived, own, three_ahead))
    own, slots_all = finish_one(own, c_factor, (one_ahead, two_ahead, three_ahead))
    one_received = exchange(own, "item")

    matrix, ones = first_half(pieces, arrived, slots_all, None)
    ones, one_received = lax.optimization_barrier((ones, one_received))
    one_total = sum_and_spread(one_received, items, ("item", "slot"), items * slots)
    inverse = second_half(matrix, ones)
    segment_raw, a_parts, mine, other = solve_one(one_total, inverse, items, slots)

    arrived = swap(other, "seg", 1)
    two, held = contraction(tensor, a_parts, c_factor, 0, 0, 8, load=True)
    arrived, two = lax.optimization_barrier((arrived, two))
    mine = mine + arrived
    arrived = swap(mine, "seg", 2)
    two, held = contraction(held, a_parts, c_factor, 0, 8, 24, (two,))
    arrived, two = lax.optimization_barrier((arrived, two))
    mine = mine + arrived
    arrived = swap(mine, "seg", 1)
    two, held = contraction(held, a_parts, c_factor, 0, 24, depth, (two,))

    two_received = exchange(two, ("seg", "slot"))
    matrix, scale = first_half(mine, arrived, slots_all, tensor.shape[1] * segs)
    scale, two_received = lax.optimization_barrier((scale, two_received))
    two_total = sum_and_spread(two_received, segs * slots, ("seg", "slot"), segs * slots)
    inverse = second_half(matrix, scale)
    a_factor = segment_raw / scale
    item_raw, squares = solve_two(two_total, scale, inverse, 8 * items)
    squares = jnp.sum(exchange(squares, "item").reshape(items, 8, width)[:, 0], axis=0)
    lambda_b = jnp.sqrt(squares / (tensor.shape[2] * items) + EPSILON)
    b_new = item_raw / lambda_b[None, :]
    return (a_factor, b_new, scale.reshape(width), lambda_b)


def solution(mesh):
    placed = (P("slot", "seg", "item"), P("item", None), P("slot", None))
    return jax.shard_map(
        local,
        mesh=mesh,
        in_specs=placed,
        out_specs=(P("seg", None), P("item", None), P(), P()),
        check_vma=False,
    )
```

```python
import functools

import jax
import jax.numpy as jnp
from jax import lax
from jax.experimental import pallas as pl
from jax.experimental.pallas import tpu as pltpu
from jax.sharding import PartitionSpec as P

RIDGE_WEIGHT = 0.1
EPSILON = 1e-06
HIGHEST = lax.Precision.HIGHEST
BLOCK = 128
PANEL = 16
GROUP = 4
VMEM = pl.BlockSpec(memory_space=pltpu.VMEM)
HBM = pl.BlockSpec(memory_space=pltpu.HBM)
PARAMS = pltpu.CompilerParams(vmem_limit_bytes=24 * 1024 * 1024)


def dot_full(left, right, left_dim=1):
    return lax.dot_general(
        left, right, (((left_dim,), (0,)), ((), ())), precision=HIGHEST, preferred_element_type=jnp.float32
    )


def dot_parts(left, right):
    return lax.dot_general(left, right, (((1,), (0,)), ((), ())), preferred_element_type=jnp.float32)


def split_two(values):
    high = values.astype(jnp.bfloat16)
    return high, (values - high.astype(jnp.float32)).astype(jnp.bfloat16)


def strip_place(strip):
    return ((0, 0), (1, 0), (1, 3 * BLOCK), (0, 4 * BLOCK))[strip]


def core_index():
    return lax.rem(lax.axis_index("seg"), 2)


def store_gram(rows, strips_ref):
    width = rows.shape[1]
    core = core_index()
    for strip in range(width // BLOCK):
        slab, start = strip_place(strip)
        low = strip * BLOCK
        place = core if slab == 0 else 1 - core
        strips_ref[place, :, start:start + width - low] = dot_full(rows[:, low:low + BLOCK], rows[:, low:], 0)


def store_parts(values, parts_ref):
    depth = values.shape[0]
    high, low = split_two(values)
    parts_ref[0:depth, :] = high
    parts_ref[depth:2 * depth, :] = high
    parts_ref[2 * depth:3 * depth, :] = low


def slab_shape(width):
    return (BLOCK, width + BLOCK)


def contraction_kernel(*refs, contract, first, last, ahead, load, ready=None):
    if load:
        source_ref, parts_ref, weight_ref, *start_refs, out_ref, tensor_ref, pieces_ref, arrived = refs
    else:
        parts_ref, weight_ref, *start_refs, tensor_ref, out_ref, unused, pieces_ref = refs
    depth = parts_ref.shape[0] // 3
    cols = tensor_ref.shape[2]
    height = tensor_ref.shape[1]
    rows = pl.ds(0, height)
    if ahead is not None:
        slots = lax.axis_size("slot")
        height = height // slots

        def quarter(distance):
            return pl.ds(pl.multiple_of(lax.rem(lax.axis_index("slot") + distance, slots) * height, height), height)

        rows = quarter(ahead)
    group = GROUP if contract == 1 else 1
    half = pieces_ref.shape[0] // 2

    waiting = {}
    if load:
        total_slots = tensor_ref.shape[0]
        if ahead is None:
            bounds = (first, first + 1, first + 3, last, (last + total_slots) // 2, total_slots)
        else:
            bounds = (0, 4, 12, total_slots)
        steps = [(rows, low, high) for low, high in zip(bounds, bounds[1:])]
        if ahead is not None:
            steps += [(quarter(ahead + distance), 0, total_slots) for distance in range(1, slots)]
        for n, (place, low, high) in enumerate(steps):
            here = (pl.ds(low, high - low), place, slice(None))
            waiting[n] = pltpu.make_async_copy(source_ref.at[here], tensor_ref.at[here], arrived.at[n])
            waiting[n].start()

    if ready is not None:
        ready()

    def prepare(k):
        for n in list(waiting):
            if steps[n][0] is rows and steps[n][1] == k:
                waiting.pop(n).wait()
        here = pl.ds(k // group % 2 * half, half)
        upper, lower = split_two(tensor_ref[k:k + group, rows, :].reshape(group * height, cols))
        pieces_ref[here, 0:depth] = upper if contract == 1 else upper.T
        pieces_ref[here, depth:2 * depth] = lower if contract == 1 else lower.T

    def product(k):
        here = pl.ds(k // group % 2 * half, half)
        return dot_parts(pieces_ref[here, :], parts_ref[0:2 * depth, :]) + dot_parts(
            pieces_ref[here, 0:depth], parts_ref[2 * depth:3 * depth, :]
        )

    size = half // group
    prepare(first)
    for k in range(first, last, group):
        if k + group < last:
            prepare(k + group)
        term = product(k)
        total = sum(term[n * size:(n + 1) * size, :] * weight_ref[k + n:k + n + 1, :] for n in range(group))
        if k == first:
            out_ref[0:size, :] = sum((ref[0:size, :] for ref in start_refs), total)
        else:
            out_ref[0:size, :] += total
    if out_ref.shape[0] > size:
        out_ref[size:, :] = weight_ref[...]
    for copy in waiting.values():
        copy.wait()


def contraction(tensor, parts, weights, contract, first, last, start=(), ahead=None, load=False):
    slots, rows, cols = tensor.shape
    width = parts.shape[1]
    height = rows if ahead is None else rows // lax.axis_size("slot")
    out_rows = height if contract == 1 else cols
    if ahead:
        out_rows += slots
    count = last - first
    kernel = functools.partial(contraction_kernel, contract=contract, first=first, last=last, ahead=ahead, load=load)
    inputs = [parts, weights, *start]
    out_shape = jax.ShapeDtypeStruct((out_rows, width), jnp.float32)
    pieces = pltpu.VMEM((2 * (GROUP * height if contract == 1 else cols), 2 * parts.shape[0] // 3), jnp.bfloat16)
    return pl.pallas_call(
        kernel,
        in_specs=[HBM] + [VMEM] * len(inputs) if load else [VMEM] * (len(inputs) + 1),
        out_specs=(VMEM, VMEM),
        out_shape=(out_shape, jax.ShapeDtypeStruct(tensor.shape, tensor.dtype)),
        scratch_shapes=[pieces] + ([pltpu.SemaphoreType.DMA((6,))] if load else []),
        input_output_aliases={} if load else {len(inputs): 1},
        compiler_params=PARAMS,
        cost_estimate=pl.CostEstimate(
            flops=10**6,
            bytes_accessed=10**4,
            transcendentals=0,
        ),
    )(*([tensor] + inputs if load else inputs + [tensor]))


def first_quarter_kernel(tensor_ref, rows_ref, slots_ref, *refs, ahead):
    *piece_refs, parts_ref, out_ref, held_ref, weight_ref, pieces_ref, arrived, strips_ref, factor_ref, fetched = refs
    copies = (
        pltpu.make_async_copy(rows_ref, factor_ref, fetched.at[0]),
        pltpu.make_async_copy(slots_ref, weight_ref, fetched.at[1]),
    )
    for copy in copies:
        copy.start()

    def ready():
        copies[0].wait()
        rows = factor_ref[...]
        store_parts(rows, parts_ref)
        store_gram(rows, strips_ref)
        along = lax.axis_index("item") // 2
        height = piece_refs[0].shape[0]
        for distance, ref in enumerate(piece_refs):
            owner = lax.rem(along + distance, len(piece_refs))
            ref[...] = strips_ref[0, pl.ds(pl.multiple_of(owner * height, height), height), :]
        copies[1].wait()

    contraction_kernel(
        tensor_ref, parts_ref, weight_ref, out_ref, held_ref, pieces_ref, arrived,
        contract=1, first=0, last=tensor_ref.shape[0], ahead=ahead, load=True, ready=ready,
    )


def first_quarter(tensor, rows, slots, ahead, count):
    depth, width = rows.shape
    height = tensor.shape[1] // lax.axis_size("slot")
    piece = jax.ShapeDtypeStruct((BLOCK // count, width + BLOCK), jnp.float32)
    out_shape = (piece,) * count + (
        jax.ShapeDtypeStruct((3 * depth, width), jnp.bfloat16),
        jax.ShapeDtypeStruct((height + slots.shape[0], width), jnp.float32),
        jax.ShapeDtypeStruct(tensor.shape, tensor.dtype),
        jax.ShapeDtypeStruct(slots.shape, slots.dtype),
    )
    return pl.pallas_call(
        functools.partial(first_quarter_kernel, ahead=ahead),
        in_specs=[HBM, HBM, HBM],
        out_specs=(VMEM,) * len(out_shape),
        out_shape=out_shape,
        scratch_shapes=[
            pltpu.VMEM((2 * GROUP * height, 2 * depth), jnp.bfloat16),
            pltpu.SemaphoreType.DMA((6,)),
            pltpu.VMEM((2, *slab_shape(width)), jnp.float32),
            pltpu.VMEM(rows.shape, jnp.float32),
            pltpu.SemaphoreType.DMA((2,)),
        ],
        compiler_params=PARAMS,
    )(tensor, rows, slots)


def finish_one_kernel(own_ref, slots_ref, *refs):
    *arrived_refs, total_ref, slots_all_ref = refs
    height, depth = own_ref.shape[0], slots_ref.shape[0]
    total_ref[...] = sum((ref[0:height, :] for ref in arrived_refs), own_ref[...])
    slots_all_ref[0:depth, :] = slots_ref[...]
    for n, ref in enumerate(arrived_refs):
        slots_all_ref[(n + 1) * depth:(n + 2) * depth, :] = ref[height:, :]


def finish_one(own, slots, arrived):
    return pl.pallas_call(
        finish_one_kernel,
        out_shape=(
            jax.ShapeDtypeStruct(own.shape, jnp.float32),
            jax.ShapeDtypeStruct((slots.shape[0] * (1 + len(arrived)), slots.shape[1]), jnp.float32),
        ),
        in_specs=[VMEM] * (2 + len(arrived)),
        out_specs=(VMEM, VMEM),
        compiler_params=PARAMS,
    )(own, slots, *arrived)


def invert_block(block):
    size = block.shape[0]
    shape = (PANEL, size)
    sub = lax.broadcasted_iota(jnp.int32, shape, 0)
    lane = lax.broadcasted_iota(jnp.int32, shape, 1)
    row_index = lax.broadcasted_iota(jnp.int32, (size, size), 0)
    col_index = lax.broadcasted_iota(jnp.int32, (size, size), 1)
    panel = block[0:PANEL, :]
    for low in range(0, size, PANEL):
        high = low + PANEL
        columns = [jnp.broadcast_to(panel[:, low + t:low + t + 1], shape) for t in range(PANEL)]
        result = jnp.where((lane >= low) & (lane < high), jnp.where(lane - low == sub, 1.0, 0.0), panel)
        for t in range(PANEL):
            here = sub == t
            column = columns[t]
            scale = 1.0 / column[t:t + 1, :]
            for u in range(t + 1, PANEL):
                pivot = columns[u][t:t + 1, :] * scale
                columns[u] = jnp.where(here, jnp.broadcast_to(pivot, shape), columns[u] - column * pivot)
            pivot = result[t:t + 1, :] * scale
            result = jnp.where(here, jnp.broadcast_to(pivot, shape), result - column * pivot)
        if high < size:
            ahead = block[high:high + PANEL, :]
            panel = jnp.where((lane >= low) & (lane < high), 0.0, ahead)
            sums = [None] * 4
            for t in range(PANEL):
                term = jnp.broadcast_to(ahead[:, low + t:low + t + 1], shape) * result[t:t + 1, :]
                sums[t % 4] = term if sums[t % 4] is None else sums[t % 4] + term
            panel = panel - ((sums[0] + sums[1]) + (sums[2] + sums[3]))
        parts = [result]
        if low:
            parts.insert(0, jnp.zeros((low, size), jnp.float32))
        if high < size:
            parts.append(jnp.zeros((size - high, size), jnp.float32))
        padded = jnp.concatenate(parts, axis=0)
        update = dot_full(block, padded)
        kept = jnp.where((col_index >= low) & (col_index < high), 0.0, block)
        block = jnp.where((row_index >= low) & (row_index < high), padded, kept - update)
    return block


def eliminate(matrix_ref, first, last):
    size = matrix_ref.shape[0]

    def step(p, carry):
        low = pl.multiple_of(p * BLOCK, BLOCK)
        here = pl.ds(low, BLOCK)
        inverse = invert_block(matrix_ref[here, here])
        column = matrix_ref[:, here]
        matrix_ref[:, here] = jnp.zeros((size, BLOCK), jnp.float32)
        matrix_ref[here, here] = jnp.eye(BLOCK, dtype=jnp.float32)
        row = dot_full(inverse, matrix_ref[here, :])
        matrix_ref[...] = matrix_ref[...] - dot_full(column, row)
        matrix_ref[here, :] = row
        return carry

    lax.fori_loop(first, last, step, 0)


def place_rows(piece_refs, strips_ref):
    core = core_index()
    item = lax.axis_index("item")
    along = item // 2
    count, height, unused = piece_refs[0].shape
    for other_core, ref in enumerate(piece_refs):
        slab = core if other_core == 0 else 1 - core
        for back in range(count):
            owner = lax.rem(along + count - back, count)
            strips_ref[slab, pl.ds(pl.multiple_of(owner * height, height), height), :] = ref[back]


def place_slabs(piece_refs, strips_ref):
    core = core_index()
    strips_ref[core] = piece_refs[0][...]
    strips_ref[1 - core] = piece_refs[1][...]


def first_half_kernel(
    mine_ref, arrived_ref, source_ref, matrix_ref, scale_ref, strips_ref, slots_ref, copied, *, rows_total
):
    copy = pltpu.make_async_copy(source_ref, slots_ref, copied)
    copy.start()
    size = matrix_ref.shape[0]
    blocks = size // BLOCK
    diagonal = lax.broadcasted_iota(jnp.int32, (BLOCK, BLOCK), 0) == lax.broadcasted_iota(
        jnp.int32, (BLOCK, BLOCK), 1
    )
    if rows_total is None:
        place_rows((mine_ref, arrived_ref), strips_ref)
        scale_ref[...] = jnp.ones_like(scale_ref)
    else:
        place_slabs((mine_ref, arrived_ref), strips_ref)
        for p in range(blocks):
            slab, start = strip_place(p)
            squares = jnp.where(diagonal, strips_ref[slab, :, start:start + BLOCK], 0.0)
            scale_ref[:, p * BLOCK:(p + 1) * BLOCK] = jnp.sqrt(
                jnp.sum(squares, axis=0, keepdims=True) / rows_total + EPSILON
            )
    copy.wait()
    slots = slots_ref[...]
    for p in range(blocks):
        slab, start = strip_place(p)
        low = p * BLOCK
        gram = strips_ref[slab, :, start:start + size - low]
        if rows_total is not None:
            squares = jnp.where(diagonal, gram[:, 0:BLOCK], 0.0)
            scale = jnp.sqrt(jnp.sum(squares, axis=1, keepdims=True) / rows_total + EPSILON)
            gram = gram / scale / scale_ref[:, low:]
        system = gram * dot_full(slots[:, low:low + BLOCK], slots[:, low:], 0)
        matrix_ref[low:low + BLOCK, low:] = system
        matrix_ref[low:low + BLOCK, low:low + BLOCK] = system[:, 0:BLOCK] + jnp.where(diagonal, RIDGE_WEIGHT, 0.0)
        for q in range(p + 1, blocks):
            matrix_ref[q * BLOCK:(q + 1) * BLOCK, low:low + BLOCK] = system[
                :, (q - p) * BLOCK:(q - p + 1) * BLOCK
            ].T
    eliminate(matrix_ref, 0, blocks // 2)


def first_half(mine, arrived, slots_all, rows_total):
    size = slots_all.shape[1]
    return pl.pallas_call(
        functools.partial(first_half_kernel, rows_total=rows_total),
        out_shape=(
            jax.ShapeDtypeStruct((size, size), jnp.float32),
            jax.ShapeDtypeStruct((1, size), jnp.float32),
        ),
        in_specs=[VMEM, VMEM, HBM],
        out_specs=(VMEM, VMEM),
        scratch_shapes=[
            pltpu.VMEM((2, *slab_shape(size)), jnp.float32),
            pltpu.VMEM(slots_all.shape, jnp.float32),
            pltpu.SemaphoreType.DMA,
        ],
        compiler_params=PARAMS,
        cost_estimate=pl.CostEstimate(flops=12 * 10**9, bytes_accessed=2**20, transcendentals=0),
    )(mine, arrived, slots_all)


def second_half_kernel(matrix_ref, *refs):
    out_ref = refs[-1]
    blocks = matrix_ref.shape[0] // BLOCK
    out_ref[...] = matrix_ref[...]
    eliminate(out_ref, blocks // 2, blocks)


def second_half(matrix, *after):
    return pl.pallas_call(
        second_half_kernel,
        out_shape=jax.ShapeDtypeStruct(matrix.shape, jnp.float32),
        in_specs=[VMEM] + [HBM] * len(after),
        out_specs=VMEM,
        input_output_aliases={0: 0},
        compiler_params=PARAMS,
        cost_estimate=pl.CostEstimate(flops=12 * 10**9, bytes_accessed=2**20, transcendentals=0),
    )(matrix, *after)


def solve_one_kernel(total_ref, inverse_ref, raw_ref, parts_ref, mine_ref, other_ref, strips_ref, *, items, slots):
    height = total_ref.shape[0] // (items * slots)
    count = items * slots
    blocks = [total_ref[n * height:(n + 1) * height, :] for z in range(slots) for n in range(z, count, slots)]
    raw = dot_full(jnp.concatenate(blocks, axis=0), inverse_ref[...])
    raw_ref[...] = raw
    store_gram(raw, strips_ref)
    mine_ref[...] = strips_ref[0]
    other_ref[...] = strips_ref[1]
    store_parts(raw, parts_ref)


def solve_one(total, inverse, items, slots):
    depth, width = total.shape
    slab = jax.ShapeDtypeStruct(slab_shape(width), jnp.float32)
    return pl.pallas_call(
        functools.partial(solve_one_kernel, items=items, slots=slots),
        out_shape=(
            jax.ShapeDtypeStruct(total.shape, jnp.float32),
            jax.ShapeDtypeStruct((3 * depth, width), jnp.bfloat16),
            slab,
            slab,
        ),
        in_specs=[VMEM, VMEM],
        out_specs=(VMEM,) * 4,
        scratch_shapes=[pltpu.VMEM((2, *slab_shape(width)), jnp.float32)],
        compiler_params=PARAMS,
    )(total, inverse)


def solve_two_kernel(total_ref, scale_ref, inverse_ref, raw_ref, squares_ref):
    raw = dot_full(total_ref[...] / scale_ref[...], inverse_ref[...])
    raw_ref[...] = raw
    squares_ref[...] = jnp.broadcast_to(jnp.sum(raw * raw, axis=0, keepdims=True), squares_ref.shape)


def solve_two(total, scale, inverse, copies):
    return pl.pallas_call(
        solve_two_kernel,
        out_shape=(
            jax.ShapeDtypeStruct(total.shape, jnp.float32),
            jax.ShapeDtypeStruct((copies, total.shape[1]), jnp.float32),
        ),
        in_specs=[VMEM, VMEM, VMEM],
        out_specs=(VMEM, VMEM),
        compiler_params=PARAMS,
    )(total, scale, inverse)


def exchange(values, axes):
    return lax.all_to_all(values, axes, 0, 0, tiled=True)


def sum_and_copy_kernel(received_ref, copies_ref, *, parts):
    height = received_ref.shape[0] // parts
    total = received_ref[0:height, :]
    for p in range(1, parts):
        total = total + received_ref[p * height:(p + 1) * height, :]
    for p in range(copies_ref.shape[0] // height):
        copies_ref[p * height:(p + 1) * height, :] = total


def sum_and_spread(received, parts, axes, copies):
    rows, cols = received.shape
    copied = pl.pallas_call(
        functools.partial(sum_and_copy_kernel, parts=parts),
        out_shape=jax.ShapeDtypeStruct((rows // parts * copies, cols), jnp.float32),
        in_specs=[VMEM],
        out_specs=VMEM,
        compiler_params=PARAMS,
    )(received)
    return exchange(copied, axes)


def swap(values, axis, mask):
    return lax.ppermute(values, axis, [(i, i ^ mask) for i in range(lax.axis_size(axis))])


def shift(values, axis, table):
    return lax.ppermute(values, axis, list(enumerate(table)))


def local(tensor, b_factor, c_factor):
    width = b_factor.shape[1]
    segs, items, slots = (lax.axis_size(name) for name in ("seg", "item", "slot"))
    depth = tensor.shape[0]

    def to_slot(value, d):
        return shift(value, "slot", [(i + d) % slots for i in range(slots)])

    def along_x(value, d):
        return shift(value, "item", [(i + 2 * d) % items for i in range(items)])

    *b_pieces, b_parts, two_ahead, held, c_rows = first_quarter(tensor, b_factor, c_factor, 2, items // 2)

    def part_one(held, c_rows, ahead):
        return contraction(held, b_parts, c_rows, 1, 0, depth, (), ahead)

    arrived = [along_x(b_pieces[d], d) for d in range(1, items // 2)]
    two_ahead = to_slot(two_ahead, 2)
    one_ahead, held = part_one(held, c_rows, 1)
    *arrived, one_ahead, two_ahead, c_rows = lax.optimization_barrier((*arrived, one_ahead, two_ahead, c_rows))
    piece = sum(arrived, b_pieces[0])
    other = swap(piece, "item", 1)
    one_ahead = to_slot(one_ahead, 1)
    three_ahead, held = part_one(held, c_rows, 3)
    other, one_ahead, three_ahead, c_rows = lax.optimization_barrier((other, one_ahead, three_ahead, c_rows))
    three_ahead = to_slot(three_ahead, 3)
    piece = piece + other
    pieces = [piece] + [along_x(piece, d) for d in range(1, items // 2)]
    own, held = part_one(held, c_rows, 0)
    *pieces, own, three_ahead = lax.optimization_barrier((*pieces, own, three_ahead))
    pieces = jnp.stack(pieces)
    arrived = swap(pieces, "seg", 1)
    own, slots_all = finish_one(own, c_rows, (one_ahead, two_ahead, three_ahead))
    one_received = exchange(own, "item")

    matrix, ones = first_half(pieces, arrived, slots_all, None)
    ones, one_received = lax.optimization_barrier((ones, one_received))
    one_total = sum_and_spread(one_received, items, ("item", "slot"), items * slots)
    inverse = second_half(matrix, ones)
    segment_raw, a_parts, mine, other = solve_one(one_total, inverse, items, slots)

    arrived = swap(other, "seg", 1)
    two, held = contraction(tensor, a_parts, c_rows, 0, 0, 12, load=True)
    arrived, two = lax.optimization_barrier((arrived, two))
    mine = mine + arrived
    arrived = swap(mine, "seg", 2)
    two, held = contraction(held, a_parts, c_rows, 0, 12, depth, (two,))
    arrived, two = lax.optimization_barrier((arrived, two))
    mine = mine + arrived
    mine, two = lax.optimization_barrier((mine, two))
    arrived = swap(mine, "seg", 1)

    two_received = exchange(two, ("seg", "slot"))
    matrix, scale = first_half(mine, arrived, slots_all, tensor.shape[1] * segs)
    scale, two_received = lax.optimization_barrier((scale, two_received))
    two_total = sum_and_spread(two_received, segs * slots, ("seg", "slot"), segs * slots)
    inverse = second_half(matrix)
    a_factor = segment_raw / scale
    item_raw, squares = solve_two(two_total, scale, inverse, 8 * items)
    squares = jnp.sum(exchange(squares, "item").reshape(items, 8, width)[:, 0], axis=0)
    lambda_b = jnp.sqrt(squares / (tensor.shape[2] * items) + EPSILON)
    b_new = item_raw / lambda_b[None, :]
    return (a_factor, b_new, scale.reshape(width), lambda_b)


def solution(mesh):
    placed = (P("slot", "seg", "item"), P("item", None), P("slot", None))
    return jax.shard_map(
        local,
        mesh=mesh,
        in_specs=placed,
        out_specs=(P("seg", None), P("item", None), P(), P()),
        check_vma=False,
    )
```

```python
import functools

import jax
import jax.numpy as jnp
from jax import lax
from jax.experimental import pallas as pl
from jax.experimental.pallas import tpu as pltpu
from jax.sharding import PartitionSpec as P

RIDGE_WEIGHT = 0.1
EPSILON = 1e-06
HIGHEST = lax.Precision.HIGHEST
BLOCK = 128
PANEL = 16
GROUP = 4
VMEM = pl.BlockSpec(memory_space=pltpu.VMEM)
HBM = pl.BlockSpec(memory_space=pltpu.HBM)
PARAMS = pltpu.CompilerParams(vmem_limit_bytes=24 * 1024 * 1024)


def dot_full(left, right, left_dim=1):
    return lax.dot_general(
        left, right, (((left_dim,), (0,)), ((), ())), precision=HIGHEST, preferred_element_type=jnp.float32
    )


def dot_parts(left, right):
    return lax.dot_general(left, right, (((1,), (0,)), ((), ())), preferred_element_type=jnp.float32)


def split_two(values):
    high = values.astype(jnp.bfloat16)
    return high, (values - high.astype(jnp.float32)).astype(jnp.bfloat16)


def strip_place(strip):
    return ((0, 0), (1, 0), (1, 3 * BLOCK), (0, 4 * BLOCK))[strip]


def core_index():
    return lax.rem(lax.axis_index("seg"), 2)


def store_gram(rows, strips_ref):
    width = rows.shape[1]
    core = core_index()
    for strip in range(width // BLOCK):
        slab, start = strip_place(strip)
        low = strip * BLOCK
        place = core if slab == 0 else 1 - core
        strips_ref[place, :, start:start + width - low] = dot_full(rows[:, low:low + BLOCK], rows[:, low:], 0)


def store_parts(values, parts_ref):
    depth = values.shape[0]
    high, low = split_two(values)
    parts_ref[0:depth, :] = high
    parts_ref[depth:2 * depth, :] = high
    parts_ref[2 * depth:3 * depth, :] = low


def slab_shape(width):
    return (BLOCK, width + BLOCK)


def contraction_kernel(*refs, contract, first, last, ahead, load, ready=None):
    if load:
        source_ref, parts_ref, weight_ref, *start_refs, out_ref, tensor_ref, pieces_ref, arrived = refs
    else:
        parts_ref, weight_ref, *start_refs, tensor_ref, out_ref, unused, pieces_ref = refs
    depth = parts_ref.shape[0] // 3
    cols = tensor_ref.shape[2]
    height = tensor_ref.shape[1]
    rows = pl.ds(0, height)
    if ahead is not None:
        slots = lax.axis_size("slot")
        height = height // slots

        def quarter(distance):
            return pl.ds(pl.multiple_of(lax.rem(lax.axis_index("slot") + distance, slots) * height, height), height)

        rows = quarter(ahead)
    group = GROUP if contract == 1 else 1
    half = pieces_ref.shape[0] // 2

    waiting = {}
    if load:
        total_slots = tensor_ref.shape[0]
        if ahead is None:
            bounds = (first, first + 1, first + 3, last, (last + total_slots) // 2, total_slots)
        else:
            bounds = (0, 4, 12, total_slots)
        steps = [(rows, low, high) for low, high in zip(bounds, bounds[1:])]
        if ahead is not None:
            steps += [(quarter(ahead + distance), 0, total_slots) for distance in range(1, slots)]
        for n, (place, low, high) in enumerate(steps):
            here = (pl.ds(low, high - low), place, slice(None))
            waiting[n] = pltpu.make_async_copy(source_ref.at[here], tensor_ref.at[here], arrived.at[n])
            waiting[n].start()

    if ready is not None:
        ready()

    def prepare(k):
        for n in list(waiting):
            if steps[n][0] is rows and steps[n][1] == k:
                waiting.pop(n).wait()
        here = pl.ds(k // group % 2 * half, half)
        upper, lower = split_two(tensor_ref[k:k + group, rows, :].reshape(group * height, cols))
        pieces_ref[here, 0:depth] = upper if contract == 1 else upper.T
        pieces_ref[here, depth:2 * depth] = lower if contract == 1 else lower.T

    def product(k):
        here = pl.ds(k // group % 2 * half, half)
        return dot_parts(pieces_ref[here, :], parts_ref[0:2 * depth, :]) + dot_parts(
            pieces_ref[here, 0:depth], parts_ref[2 * depth:3 * depth, :]
        )

    size = half // group
    prepare(first)
    for k in range(first, last, group):
        if k + group < last:
            prepare(k + group)
        term = product(k)
        total = sum(term[n * size:(n + 1) * size, :] * weight_ref[k + n:k + n + 1, :] for n in range(group))
        if k == first:
            out_ref[0:size, :] = sum((ref[0:size, :] for ref in start_refs), total)
        else:
            out_ref[0:size, :] += total
    if out_ref.shape[0] > size:
        out_ref[size:, :] = weight_ref[...]
    for copy in waiting.values():
        copy.wait()


def contraction(tensor, parts, weights, contract, first, last, start=(), ahead=None, load=False):
    slots, rows, cols = tensor.shape
    width = parts.shape[1]
    height = rows if ahead is None else rows // lax.axis_size("slot")
    out_rows = height if contract == 1 else cols
    if ahead:
        out_rows += slots
    count = last - first
    kernel = functools.partial(contraction_kernel, contract=contract, first=first, last=last, ahead=ahead, load=load)
    inputs = [parts, weights, *start]
    out_shape = jax.ShapeDtypeStruct((out_rows, width), jnp.float32)
    pieces = pltpu.VMEM((2 * (GROUP * height if contract == 1 else cols), 2 * parts.shape[0] // 3), jnp.bfloat16)
    return pl.pallas_call(
        kernel,
        in_specs=[HBM] + [VMEM] * len(inputs) if load else [VMEM] * (len(inputs) + 1),
        out_specs=(VMEM, VMEM),
        out_shape=(out_shape, jax.ShapeDtypeStruct(tensor.shape, tensor.dtype)),
        scratch_shapes=[pieces] + ([pltpu.SemaphoreType.DMA((6,))] if load else []),
        input_output_aliases={} if load else {len(inputs): 1},
        compiler_params=PARAMS,
        cost_estimate=pl.CostEstimate(
            flops=10**6,
            bytes_accessed=10**4,
            transcendentals=0,
        ),
    )(*([tensor] + inputs if load else inputs + [tensor]))


def first_quarter_kernel(tensor_ref, rows_ref, slots_ref, *refs, ahead):
    *piece_refs, parts_ref, out_ref, held_ref, weight_ref, pieces_ref, arrived, strips_ref, factor_ref, fetched = refs
    copies = (
        pltpu.make_async_copy(rows_ref, factor_ref, fetched.at[0]),
        pltpu.make_async_copy(slots_ref, weight_ref, fetched.at[1]),
    )
    for copy in copies:
        copy.start()

    def ready():
        copies[0].wait()
        rows = factor_ref[...]
        store_parts(rows, parts_ref)
        store_gram(rows, strips_ref)
        along = lax.axis_index("item") // 2
        height = piece_refs[0].shape[0]
        for distance, ref in enumerate(piece_refs):
            owner = lax.rem(along + distance, len(piece_refs))
            ref[...] = strips_ref[0, pl.ds(pl.multiple_of(owner * height, height), height), :]
        copies[1].wait()

    contraction_kernel(
        tensor_ref, parts_ref, weight_ref, out_ref, held_ref, pieces_ref, arrived,
        contract=1, first=0, last=tensor_ref.shape[0], ahead=ahead, load=True, ready=ready,
    )


def first_quarter(tensor, rows, slots, ahead, count):
    depth, width = rows.shape
    height = tensor.shape[1] // lax.axis_size("slot")
    piece = jax.ShapeDtypeStruct((BLOCK // count, width + BLOCK), jnp.float32)
    out_shape = (piece,) * count + (
        jax.ShapeDtypeStruct((3 * depth, width), jnp.bfloat16),
        jax.ShapeDtypeStruct((height + slots.shape[0], width), jnp.float32),
        jax.ShapeDtypeStruct(tensor.shape, tensor.dtype),
        jax.ShapeDtypeStruct(slots.shape, slots.dtype),
    )
    return pl.pallas_call(
        functools.partial(first_quarter_kernel, ahead=ahead),
        in_specs=[HBM, HBM, HBM],
        out_specs=(VMEM,) * len(out_shape),
        out_shape=out_shape,
        scratch_shapes=[
            pltpu.VMEM((2 * GROUP * height, 2 * depth), jnp.bfloat16),
            pltpu.SemaphoreType.DMA((6,)),
            pltpu.VMEM((2, *slab_shape(width)), jnp.float32),
            pltpu.VMEM(rows.shape, jnp.float32),
            pltpu.SemaphoreType.DMA((2,)),
        ],
        compiler_params=PARAMS,
    )(tensor, rows, slots)


def finish_one_kernel(own_ref, slots_ref, *refs):
    *arrived_refs, total_ref, slots_all_ref = refs
    height, depth = own_ref.shape[0], slots_ref.shape[0]
    total_ref[...] = sum((ref[0:height, :] for ref in arrived_refs), own_ref[...])
    slots_all_ref[0:depth, :] = slots_ref[...]
    for n, ref in enumerate(arrived_refs):
        slots_all_ref[(n + 1) * depth:(n + 2) * depth, :] = ref[height:, :]


def finish_one(own, slots, arrived):
    return pl.pallas_call(
        finish_one_kernel,
        out_shape=(
            jax.ShapeDtypeStruct(own.shape, jnp.float32),
            jax.ShapeDtypeStruct((slots.shape[0] * (1 + len(arrived)), slots.shape[1]), jnp.float32),
        ),
        in_specs=[VMEM] * (2 + len(arrived)),
        out_specs=(VMEM, VMEM),
        compiler_params=PARAMS,
    )(own, slots, *arrived)


def invert_block(block):
    size = block.shape[0]
    shape = (PANEL, size)
    sub = lax.broadcasted_iota(jnp.int32, shape, 0)
    lane = lax.broadcasted_iota(jnp.int32, shape, 1)
    row_index = lax.broadcasted_iota(jnp.int32, (size, size), 0)
    col_index = lax.broadcasted_iota(jnp.int32, (size, size), 1)
    panel = block[0:PANEL, :]
    for low in range(0, size, PANEL):
        high = low + PANEL
        columns = [jnp.broadcast_to(panel[:, low + t:low + t + 1], shape) for t in range(PANEL)]
        result = jnp.where((lane >= low) & (lane < high), jnp.where(lane - low == sub, 1.0, 0.0), panel)
        for t in range(PANEL):
            here = sub == t
            column = columns[t]
            scale = 1.0 / column[t:t + 1, :]
            for u in range(t + 1, PANEL):
                pivot = columns[u][t:t + 1, :] * scale
                columns[u] = jnp.where(here, jnp.broadcast_to(pivot, shape), columns[u] - column * pivot)
            pivot = result[t:t + 1, :] * scale
            result = jnp.where(here, jnp.broadcast_to(pivot, shape), result - column * pivot)
        if high < size:
            ahead = block[high:high + PANEL, :]
            panel = jnp.where((lane >= low) & (lane < high), 0.0, ahead)
            sums = [None] * 4
            for t in range(PANEL):
                term = jnp.broadcast_to(ahead[:, low + t:low + t + 1], shape) * result[t:t + 1, :]
                sums[t % 4] = term if sums[t % 4] is None else sums[t % 4] + term
            panel = panel - ((sums[0] + sums[1]) + (sums[2] + sums[3]))
        parts = [result]
        if low:
            parts.insert(0, jnp.zeros((low, size), jnp.float32))
        if high < size:
            parts.append(jnp.zeros((size - high, size), jnp.float32))
        padded = jnp.concatenate(parts, axis=0)
        update = dot_full(block, padded)
        kept = jnp.where((col_index >= low) & (col_index < high), 0.0, block)
        block = jnp.where((row_index >= low) & (row_index < high), padded, kept - update)
    return block


def eliminate(matrix_ref, first, last):
    size = matrix_ref.shape[0]

    def step(p, carry):
        low = pl.multiple_of(p * BLOCK, BLOCK)
        here = pl.ds(low, BLOCK)
        inverse = invert_block(matrix_ref[here, here])
        column = matrix_ref[:, here]
        matrix_ref[:, here] = jnp.zeros((size, BLOCK), jnp.float32)
        matrix_ref[here, here] = jnp.eye(BLOCK, dtype=jnp.float32)
        row = dot_full(inverse, matrix_ref[here, :])
        matrix_ref[...] = matrix_ref[...] - dot_full(column, row)
        matrix_ref[here, :] = row
        return carry

    lax.fori_loop(first, last, step, 0)


def place_rows(piece_refs, strips_ref):
    core = core_index()
    item = lax.axis_index("item")
    along = item // 2
    count, height, unused = piece_refs[0].shape
    for other_core, ref in enumerate(piece_refs):
        slab = core if other_core == 0 else 1 - core
        for back in range(count):
            owner = lax.rem(along + count - back, count)
            strips_ref[slab, pl.ds(pl.multiple_of(owner * height, height), height), :] = ref[back]


def place_slabs(piece_refs, strips_ref):
    core = core_index()
    strips_ref[core] = piece_refs[0][...]
    strips_ref[1 - core] = piece_refs[1][...]


def first_half_kernel(
    mine_ref, arrived_ref, source_ref, matrix_ref, scale_ref, strips_ref, slots_ref, copied, *, rows_total, done
):
    copy = pltpu.make_async_copy(source_ref, slots_ref, copied)
    copy.start()
    size = matrix_ref.shape[0]
    blocks = size // BLOCK
    diagonal = lax.broadcasted_iota(jnp.int32, (BLOCK, BLOCK), 0) == lax.broadcasted_iota(
        jnp.int32, (BLOCK, BLOCK), 1
    )
    if rows_total is None:
        place_rows((mine_ref, arrived_ref), strips_ref)
        scale_ref[...] = jnp.ones_like(scale_ref)
    else:
        place_slabs((mine_ref, arrived_ref), strips_ref)
        for p in range(blocks):
            slab, start = strip_place(p)
            squares = jnp.where(diagonal, strips_ref[slab, :, start:start + BLOCK], 0.0)
            scale_ref[:, p * BLOCK:(p + 1) * BLOCK] = jnp.sqrt(
                jnp.sum(squares, axis=0, keepdims=True) / rows_total + EPSILON
            )
    copy.wait()
    slots = slots_ref[...]
    for p in range(blocks):
        slab, start = strip_place(p)
        low = p * BLOCK
        gram = strips_ref[slab, :, start:start + size - low]
        if rows_total is not None:
            squares = jnp.where(diagonal, gram[:, 0:BLOCK], 0.0)
            scale = jnp.sqrt(jnp.sum(squares, axis=1, keepdims=True) / rows_total + EPSILON)
            gram = gram / scale / scale_ref[:, low:]
        system = gram * dot_full(slots[:, low:low + BLOCK], slots[:, low:], 0)
        matrix_ref[low:low + BLOCK, low:] = system
        matrix_ref[low:low + BLOCK, low:low + BLOCK] = system[:, 0:BLOCK] + jnp.where(diagonal, RIDGE_WEIGHT, 0.0)
        for q in range(p + 1, blocks):
            matrix_ref[q * BLOCK:(q + 1) * BLOCK, low:low + BLOCK] = system[
                :, (q - p) * BLOCK:(q - p + 1) * BLOCK
            ].T
    eliminate(matrix_ref, 0, done)


def first_half(mine, arrived, slots_all, rows_total, done):
    size = slots_all.shape[1]
    return pl.pallas_call(
        functools.partial(first_half_kernel, rows_total=rows_total, done=done),
        out_shape=(
            jax.ShapeDtypeStruct((size, size), jnp.float32),
            jax.ShapeDtypeStruct((1, size), jnp.float32),
        ),
        in_specs=[VMEM, VMEM, HBM],
        out_specs=(VMEM, VMEM),
        scratch_shapes=[
            pltpu.VMEM((2, *slab_shape(size)), jnp.float32),
            pltpu.VMEM(slots_all.shape, jnp.float32),
            pltpu.SemaphoreType.DMA,
        ],
        compiler_params=PARAMS,
        cost_estimate=pl.CostEstimate(flops=12 * 10**9, bytes_accessed=2**20, transcendentals=0),
    )(mine, arrived, slots_all)


def second_half_kernel(matrix_ref, *refs, done):
    out_ref = refs[-1]
    blocks = matrix_ref.shape[0] // BLOCK
    out_ref[...] = matrix_ref[...]
    eliminate(out_ref, done, blocks)


def second_half(matrix, done, *after):
    return pl.pallas_call(
        functools.partial(second_half_kernel, done=done),
        out_shape=jax.ShapeDtypeStruct(matrix.shape, jnp.float32),
        in_specs=[VMEM] + [HBM] * len(after),
        out_specs=VMEM,
        input_output_aliases={0: 0},
        compiler_params=PARAMS,
        cost_estimate=pl.CostEstimate(flops=12 * 10**9, bytes_accessed=2**20, transcendentals=0),
    )(matrix, *after)


def solve_one_kernel(tensor_ref, total_ref, inverse_ref, weight_ref, *refs, items, slots, last):
    raw_ref, parts_ref, mine_ref, other_ref, out_ref, held_ref, pieces_ref, arrived, strips_ref = refs

    def ready():
        height = total_ref.shape[0] // (items * slots)
        count = items * slots
        blocks = [total_ref[n * height:(n + 1) * height, :] for z in range(slots) for n in range(z, count, slots)]
        raw = dot_full(jnp.concatenate(blocks, axis=0), inverse_ref[...])
        raw_ref[...] = raw
        store_gram(raw, strips_ref)
        mine_ref[...] = strips_ref[0]
        other_ref[...] = strips_ref[1]
        store_parts(raw, parts_ref)

    contraction_kernel(
        tensor_ref, parts_ref, weight_ref, out_ref, held_ref, pieces_ref, arrived,
        contract=0, first=0, last=last, ahead=None, load=True, ready=ready,
    )


def solve_one(tensor, total, inverse, weights, items, slots, last):
    depth, width = total.shape
    cols = tensor.shape[2]
    slab = jax.ShapeDtypeStruct(slab_shape(width), jnp.float32)
    out_shape = (
        jax.ShapeDtypeStruct(total.shape, jnp.float32),
        jax.ShapeDtypeStruct((3 * depth, width), jnp.bfloat16),
        slab,
        slab,
        jax.ShapeDtypeStruct((cols, width), jnp.float32),
        jax.ShapeDtypeStruct(tensor.shape, tensor.dtype),
    )
    return pl.pallas_call(
        functools.partial(solve_one_kernel, items=items, slots=slots, last=last),
        out_shape=out_shape,
        in_specs=[HBM, VMEM, VMEM, VMEM],
        out_specs=(VMEM,) * len(out_shape),
        scratch_shapes=[
            pltpu.VMEM((2 * cols, 2 * depth), jnp.bfloat16),
            pltpu.SemaphoreType.DMA((6,)),
            pltpu.VMEM((2, *slab_shape(width)), jnp.float32),
        ],
        compiler_params=PARAMS,
    )(tensor, total, inverse, weights)


def solve_two_kernel(total_ref, scale_ref, inverse_ref, raw_ref, squares_ref):
    raw = dot_full(total_ref[...] / scale_ref[...], inverse_ref[...])
    raw_ref[...] = raw
    squares_ref[...] = jnp.broadcast_to(jnp.sum(raw * raw, axis=0, keepdims=True), squares_ref.shape)


def solve_two(total, scale, inverse, copies):
    return pl.pallas_call(
        solve_two_kernel,
        out_shape=(
            jax.ShapeDtypeStruct(total.shape, jnp.float32),
            jax.ShapeDtypeStruct((copies, total.shape[1]), jnp.float32),
        ),
        in_specs=[VMEM, VMEM, VMEM],
        out_specs=(VMEM, VMEM),
        compiler_params=PARAMS,
    )(total, scale, inverse)


def exchange(values, axes):
    return lax.all_to_all(values, axes, 0, 0, tiled=True)


def sum_and_copy_kernel(received_ref, copies_ref, *, parts):
    height = received_ref.shape[0] // parts
    total = received_ref[0:height, :]
    for p in range(1, parts):
        total = total + received_ref[p * height:(p + 1) * height, :]
    for p in range(copies_ref.shape[0] // height):
        copies_ref[p * height:(p + 1) * height, :] = total


def sum_and_spread(received, parts, axes, copies):
    rows, cols = received.shape
    copied = pl.pallas_call(
        functools.partial(sum_and_copy_kernel, parts=parts),
        out_shape=jax.ShapeDtypeStruct((rows // parts * copies, cols), jnp.float32),
        in_specs=[VMEM],
        out_specs=VMEM,
        compiler_params=PARAMS,
    )(received)
    return exchange(copied, axes)


def swap(values, axis, mask):
    return lax.ppermute(values, axis, [(i, i ^ mask) for i in range(lax.axis_size(axis))])


def shift(values, axis, table):
    return lax.ppermute(values, axis, list(enumerate(table)))


def local(tensor, b_factor, c_factor):
    width = b_factor.shape[1]
    segs, items, slots = (lax.axis_size(name) for name in ("seg", "item", "slot"))
    depth = tensor.shape[0]

    def to_slot(value, d):
        return shift(value, "slot", [(i + d) % slots for i in range(slots)])

    def along_x(value, d):
        return shift(value, "item", [(i + 2 * d) % items for i in range(items)])

    *b_pieces, b_parts, one_ahead, held, c_rows = first_quarter(tensor, b_factor, c_factor, 1, items // 2)

    def part_one(held, c_rows, ahead):
        return contraction(held, b_parts, c_rows, 1, 0, depth, (), ahead)

    arrived = [along_x(b_pieces[d], d) for d in range(1, items // 2)]
    one_ahead = to_slot(one_ahead, 1)
    two_ahead, held = part_one(held, c_rows, 2)
    *arrived, one_ahead, two_ahead, c_rows = lax.optimization_barrier((*arrived, one_ahead, two_ahead, c_rows))
    piece = sum(arrived, b_pieces[0])
    other = swap(piece, "item", 1)
    two_ahead = to_slot(two_ahead, 2)
    three_ahead, held = part_one(held, c_rows, 3)
    other, three_ahead = lax.optimization_barrier((other, three_ahead))
    three_ahead = to_slot(three_ahead, 3)
    piece = piece + other
    pieces = [piece] + [along_x(piece, d) for d in range(1, items // 2)]
    two_ahead, c_rows = lax.optimization_barrier((two_ahead, c_rows))
    own, held = part_one(held, c_rows, 0)
    *pieces, own, three_ahead = lax.optimization_barrier((*pieces, own, three_ahead))
    pieces = jnp.stack(pieces)
    arrived = swap(pieces, "seg", 1)
    own, slots_all = finish_one(own, c_rows, (one_ahead, two_ahead, three_ahead))
    one_received = exchange(own, "item")

    matrix, ones = first_half(pieces, arrived, slots_all, None, 1)
    ones, one_received = lax.optimization_barrier((ones, one_received))
    one_total = sum_and_spread(one_received, items, ("item", "slot"), items * slots)
    inverse = second_half(matrix, 1, ones)
    segment_raw, a_parts, mine, other, two, held = solve_one(tensor, one_total, inverse, c_rows, items, slots, 4)

    arrived = swap(other, "seg", 1)
    two, held = contraction(held, a_parts, c_rows, 0, 4, 12, (two,))
    arrived, two = lax.optimization_barrier((arrived, two))
    mine = mine + arrived
    arrived = swap(mine, "seg", 2)
    two, held = contraction(held, a_parts, c_rows, 0, 12, depth, (two,))
    arrived, two = lax.optimization_barrier((arrived, two))
    mine = mine + arrived
    mine, two = lax.optimization_barrier((mine, two))
    arrived = swap(mine, "seg", 1)

    two_received = exchange(two, ("seg", "slot"))
    matrix, scale = first_half(mine, arrived, slots_all, tensor.shape[1] * segs, 2)
    scale, two_received = lax.optimization_barrier((scale, two_received))
    two_total = sum_and_spread(two_received, segs * slots, ("seg", "slot"), segs * slots)
    inverse = second_half(matrix, 2)
    a_factor = segment_raw / scale
    item_raw, squares = solve_two(two_total, scale, inverse, 8 * items)
    squares = jnp.sum(exchange(squares, "item").reshape(items, 8, width)[:, 0], axis=0)
    lambda_b = jnp.sqrt(squares / (tensor.shape[2] * items) + EPSILON)
    b_new = item_raw / lambda_b[None, :]
    return (a_factor, b_new, scale.reshape(width), lambda_b)


def solution(mesh):
    placed = (P("slot", "seg", "item"), P("item", None), P("slot", None))
    return jax.shard_map(
        local,
        mesh=mesh,
        in_specs=placed,
        out_specs=(P("seg", None), P("item", None), P(), P()),
        check_vma=False,
    )
```

```python
import functools

import jax
import jax.numpy as jnp
from jax import lax
from jax.experimental import pallas as pl
from jax.experimental.pallas import tpu as pltpu
from jax.sharding import PartitionSpec as P

RIDGE_WEIGHT = 0.1
EPSILON = 1e-06
HIGHEST = lax.Precision.HIGHEST
BLOCK = 128
PANEL = 16
GROUP = 4
VMEM = pl.BlockSpec(memory_space=pltpu.VMEM)
HBM = pl.BlockSpec(memory_space=pltpu.HBM)
PARAMS = pltpu.CompilerParams(vmem_limit_bytes=24 * 1024 * 1024)


def dot_full(left, right, left_dim=1):
    return lax.dot_general(
        left, right, (((left_dim,), (0,)), ((), ())), precision=HIGHEST, preferred_element_type=jnp.float32
    )


def dot_parts(left, right):
    return lax.dot_general(left, right, (((1,), (0,)), ((), ())), preferred_element_type=jnp.float32)


def split_two(values):
    high = values.astype(jnp.bfloat16)
    return high, (values - high.astype(jnp.float32)).astype(jnp.bfloat16)


def strip_place(strip):
    return ((0, 0), (1, 0), (1, 3 * BLOCK), (0, 4 * BLOCK))[strip]


def core_index():
    return lax.rem(lax.axis_index("seg"), 2)


def store_gram(rows, strips_ref):
    width = rows.shape[1]
    core = core_index()
    for strip in range(width // BLOCK):
        slab, start = strip_place(strip)
        low = strip * BLOCK
        place = core if slab == 0 else 1 - core
        strips_ref[place, :, start:start + width - low] = dot_full(rows[:, low:low + BLOCK], rows[:, low:], 0)


def store_parts(values, parts_ref):
    depth = values.shape[0]
    high, low = split_two(values)
    parts_ref[0:depth, :] = high
    parts_ref[depth:2 * depth, :] = high
    parts_ref[2 * depth:3 * depth, :] = low


def slab_shape(width):
    return (BLOCK, width + BLOCK)


def contraction_kernel(*refs, contract, first, last, ahead, load, ready=None):
    if load == "first":
        source_ref, parts_ref, weight_ref, *start_refs, out_ref, tensor_ref, pieces_ref, arrived = refs
        filled_ref = tensor_ref
    elif load == "rest":
        source_ref, parts_ref, weight_ref, *start_refs, tensor_ref, out_ref, filled_ref, pieces_ref, arrived = refs
    else:
        parts_ref, weight_ref, *start_refs, tensor_ref, out_ref, unused, pieces_ref = refs
    depth = parts_ref.shape[0] // 3
    cols = tensor_ref.shape[2]
    height = tensor_ref.shape[1]
    rows = pl.ds(0, height)
    if ahead is not None:
        slots = lax.axis_size("slot")
        height = height // slots

        def quarter(distance):
            return pl.ds(pl.multiple_of(lax.rem(lax.axis_index("slot") + distance, slots) * height, height), height)

        rows = quarter(ahead)
    group = GROUP if contract == 1 else 1
    half = pieces_ref.shape[0] // 2

    waiting = {}
    total_slots = tensor_ref.shape[0]
    if load == "first":
        if ahead is None:
            bounds = (first, first + 1, first + 3, last, last + 8)
            steps = [(rows, low, high) for low, high in zip(bounds, bounds[1:])]
        else:
            steps = [(rows, low, high) for low, high in ((0, 4), (4, 12), (12, total_slots))]
            steps += [(quarter(ahead + 1), 0, total_slots)]
    elif load == "rest":
        if ahead is None:
            steps = [(rows, last, total_slots)]
        else:
            steps = [(quarter(ahead + distance), 0, total_slots) for distance in range(1, slots - 1)]
    if load:
        for n, (place, low, high) in enumerate(steps):
            here = (pl.ds(low, high - low), place, slice(None))
            waiting[n] = pltpu.make_async_copy(source_ref.at[here], filled_ref.at[here], arrived.at[n])
            waiting[n].start()

    if ready is not None:
        ready()

    def prepare(k):
        for n in list(waiting):
            if load == "first" and steps[n][0] is rows and steps[n][1] == k:
                waiting.pop(n).wait()
        here = pl.ds(k // group % 2 * half, half)
        upper, lower = split_two(tensor_ref[k:k + group, rows, :].reshape(group * height, cols))
        pieces_ref[here, 0:depth] = upper if contract == 1 else upper.T
        pieces_ref[here, depth:2 * depth] = lower if contract == 1 else lower.T

    def product(k):
        here = pl.ds(k // group % 2 * half, half)
        return dot_parts(pieces_ref[here, :], parts_ref[0:2 * depth, :]) + dot_parts(
            pieces_ref[here, 0:depth], parts_ref[2 * depth:3 * depth, :]
        )

    size = half // group
    prepare(first)
    for k in range(first, last, group):
        if k + group < last:
            prepare(k + group)
        term = product(k)
        total = sum(term[n * size:(n + 1) * size, :] * weight_ref[k + n:k + n + 1, :] for n in range(group))
        if k == first:
            out_ref[0:size, :] = sum((ref[0:size, :] for ref in start_refs), total)
        else:
            out_ref[0:size, :] += total
    if out_ref.shape[0] > size:
        out_ref[size:, :] = weight_ref[...]
    for copy in waiting.values():
        copy.wait()


def contraction(held, parts, weights, contract, first, last, start=(), ahead=None, source=None):
    slots, rows, cols = held.shape
    width = parts.shape[1]
    height = rows if ahead is None else rows // lax.axis_size("slot")
    out_rows = height if contract == 1 else cols
    if ahead:
        out_rows += slots
    load = None if source is None else "rest"
    kernel = functools.partial(contraction_kernel, contract=contract, first=first, last=last, ahead=ahead, load=load)
    inputs = [parts, weights, *start, held]
    out_shape = jax.ShapeDtypeStruct((out_rows, width), jnp.float32)
    pieces = pltpu.VMEM((2 * (GROUP * height if contract == 1 else cols), 2 * parts.shape[0] // 3), jnp.bfloat16)
    sources = [source] if load else []
    return pl.pallas_call(
        kernel,
        in_specs=[HBM] * len(sources) + [VMEM] * len(inputs),
        out_specs=(VMEM, VMEM),
        out_shape=(out_shape, jax.ShapeDtypeStruct(held.shape, held.dtype)),
        scratch_shapes=[pieces] + ([pltpu.SemaphoreType.DMA((6,))] if load else []),
        input_output_aliases={len(sources) + len(inputs) - 1: 1},
        compiler_params=PARAMS,
        cost_estimate=pl.CostEstimate(flops=10**6, bytes_accessed=10**4, transcendentals=0),
    )(*sources, *inputs)


def first_quarter_kernel(tensor_ref, rows_ref, slots_ref, *refs, ahead):
    *piece_refs, parts_ref, out_ref, held_ref, weight_ref, pieces_ref, arrived, strips_ref, factor_ref, fetched = refs
    copies = (
        pltpu.make_async_copy(rows_ref, factor_ref, fetched.at[0]),
        pltpu.make_async_copy(slots_ref, weight_ref, fetched.at[1]),
    )
    for copy in copies:
        copy.start()

    def ready():
        copies[0].wait()
        rows = factor_ref[...]
        store_parts(rows, parts_ref)
        store_gram(rows, strips_ref)
        along = lax.axis_index("item") // 2
        height = piece_refs[0].shape[0]
        for distance, ref in enumerate(piece_refs):
            owner = lax.rem(along + distance, len(piece_refs))
            ref[...] = strips_ref[0, pl.ds(pl.multiple_of(owner * height, height), height), :]
        copies[1].wait()

    contraction_kernel(
        tensor_ref, parts_ref, weight_ref, out_ref, held_ref, pieces_ref, arrived,
        contract=1, first=0, last=tensor_ref.shape[0], ahead=ahead, load="first", ready=ready,
    )


def first_quarter(tensor, rows, slots, ahead, count):
    depth, width = rows.shape
    height = tensor.shape[1] // lax.axis_size("slot")
    piece = jax.ShapeDtypeStruct((BLOCK // count, width + BLOCK), jnp.float32)
    out_shape = (piece,) * count + (
        jax.ShapeDtypeStruct((3 * depth, width), jnp.bfloat16),
        jax.ShapeDtypeStruct((height + slots.shape[0], width), jnp.float32),
        jax.ShapeDtypeStruct(tensor.shape, tensor.dtype),
        jax.ShapeDtypeStruct(slots.shape, slots.dtype),
    )
    return pl.pallas_call(
        functools.partial(first_quarter_kernel, ahead=ahead),
        in_specs=[HBM, HBM, HBM],
        out_specs=(VMEM,) * len(out_shape),
        out_shape=out_shape,
        scratch_shapes=[
            pltpu.VMEM((2 * GROUP * height, 2 * depth), jnp.bfloat16),
            pltpu.SemaphoreType.DMA((6,)),
            pltpu.VMEM((2, *slab_shape(width)), jnp.float32),
            pltpu.VMEM(rows.shape, jnp.float32),
            pltpu.SemaphoreType.DMA((2,)),
        ],
        compiler_params=PARAMS,
    )(tensor, rows, slots)


def finish_one_kernel(own_ref, slots_ref, *refs):
    *arrived_refs, total_ref, slots_all_ref = refs
    height, depth = own_ref.shape[0], slots_ref.shape[0]
    total_ref[...] = sum((ref[0:height, :] for ref in arrived_refs), own_ref[...])
    slots_all_ref[0:depth, :] = slots_ref[...]
    for n, ref in enumerate(arrived_refs):
        slots_all_ref[(n + 1) * depth:(n + 2) * depth, :] = ref[height:, :]


def finish_one(own, slots, arrived):
    return pl.pallas_call(
        finish_one_kernel,
        out_shape=(
            jax.ShapeDtypeStruct(own.shape, jnp.float32),
            jax.ShapeDtypeStruct((slots.shape[0] * (1 + len(arrived)), slots.shape[1]), jnp.float32),
        ),
        in_specs=[VMEM] * (2 + len(arrived)),
        out_specs=(VMEM, VMEM),
        compiler_params=PARAMS,
    )(own, slots, *arrived)


def invert_block(block):
    size = block.shape[0]
    shape = (PANEL, size)
    sub = lax.broadcasted_iota(jnp.int32, shape, 0)
    lane = lax.broadcasted_iota(jnp.int32, shape, 1)
    row_index = lax.broadcasted_iota(jnp.int32, (size, size), 0)
    col_index = lax.broadcasted_iota(jnp.int32, (size, size), 1)
    panel = block[0:PANEL, :]
    for low in range(0, size, PANEL):
        high = low + PANEL
        columns = [jnp.broadcast_to(panel[:, low + t:low + t + 1], shape) for t in range(PANEL)]
        result = jnp.where((lane >= low) & (lane < high), jnp.where(lane - low == sub, 1.0, 0.0), panel)
        for t in range(PANEL):
            here = sub == t
            column = columns[t]
            scale = 1.0 / column[t:t + 1, :]
            for u in range(t + 1, PANEL):
                pivot = columns[u][t:t + 1, :] * scale
                columns[u] = jnp.where(here, jnp.broadcast_to(pivot, shape), columns[u] - column * pivot)
            pivot = result[t:t + 1, :] * scale
            result = jnp.where(here, jnp.broadcast_to(pivot, shape), result - column * pivot)
        if high < size:
            ahead = block[high:high + PANEL, :]
            panel = jnp.where((lane >= low) & (lane < high), 0.0, ahead)
            sums = [None] * 4
            for t in range(PANEL):
                term = jnp.broadcast_to(ahead[:, low + t:low + t + 1], shape) * result[t:t + 1, :]
                sums[t % 4] = term if sums[t % 4] is None else sums[t % 4] + term
            panel = panel - ((sums[0] + sums[1]) + (sums[2] + sums[3]))
        parts = [result]
        if low:
            parts.insert(0, jnp.zeros((low, size), jnp.float32))
        if high < size:
            parts.append(jnp.zeros((size - high, size), jnp.float32))
        padded = jnp.concatenate(parts, axis=0)
        update = dot_full(block, padded)
        kept = jnp.where((col_index >= low) & (col_index < high), 0.0, block)
        block = jnp.where((row_index >= low) & (row_index < high), padded, kept - update)
    return block


def eliminate(matrix_ref, first, last):
    size = matrix_ref.shape[0]

    def step(p, carry):
        low = pl.multiple_of(p * BLOCK, BLOCK)
        here = pl.ds(low, BLOCK)
        inverse = invert_block(matrix_ref[here, here])
        column = matrix_ref[:, here]
        matrix_ref[:, here] = jnp.zeros((size, BLOCK), jnp.float32)
        matrix_ref[here, here] = jnp.eye(BLOCK, dtype=jnp.float32)
        row = dot_full(inverse, matrix_ref[here, :])
        matrix_ref[...] = matrix_ref[...] - dot_full(column, row)
        matrix_ref[here, :] = row
        return carry

    lax.fori_loop(first, last, step, 0)


def place_rows(piece_refs, strips_ref):
    core = core_index()
    item = lax.axis_index("item")
    along = item // 2
    count, height, unused = piece_refs[0].shape
    for other_core, ref in enumerate(piece_refs):
        slab = core if other_core == 0 else 1 - core
        for back in range(count):
            owner = lax.rem(along + count - back, count)
            strips_ref[slab, pl.ds(pl.multiple_of(owner * height, height), height), :] = ref[back]


def place_slabs(piece_refs, strips_ref):
    core = core_index()
    strips_ref[core] = piece_refs[0][...]
    strips_ref[1 - core] = piece_refs[1][...]


def first_half_kernel(
    mine_ref, arrived_ref, source_ref, matrix_ref, scale_ref, strips_ref, slots_ref, copied, *, rows_total, done
):
    copy = pltpu.make_async_copy(source_ref, slots_ref, copied)
    copy.start()
    size = matrix_ref.shape[0]
    blocks = size // BLOCK
    diagonal = lax.broadcasted_iota(jnp.int32, (BLOCK, BLOCK), 0) == lax.broadcasted_iota(
        jnp.int32, (BLOCK, BLOCK), 1
    )
    if rows_total is None:
        place_rows((mine_ref, arrived_ref), strips_ref)
        scale_ref[...] = jnp.ones_like(scale_ref)
    else:
        place_slabs((mine_ref, arrived_ref), strips_ref)
        for p in range(blocks):
            slab, start = strip_place(p)
            squares = jnp.where(diagonal, strips_ref[slab, :, start:start + BLOCK], 0.0)
            scale_ref[:, p * BLOCK:(p + 1) * BLOCK] = jnp.sqrt(
                jnp.sum(squares, axis=0, keepdims=True) / rows_total + EPSILON
            )
    copy.wait()
    slots = slots_ref[...]
    for p in range(blocks):
        slab, start = strip_place(p)
        low = p * BLOCK
        gram = strips_ref[slab, :, start:start + size - low]
        if rows_total is not None:
            squares = jnp.where(diagonal, gram[:, 0:BLOCK], 0.0)
            scale = jnp.sqrt(jnp.sum(squares, axis=1, keepdims=True) / rows_total + EPSILON)
            gram = gram / scale / scale_ref[:, low:]
        system = gram * dot_full(slots[:, low:low + BLOCK], slots[:, low:], 0)
        matrix_ref[low:low + BLOCK, low:] = system
        matrix_ref[low:low + BLOCK, low:low + BLOCK] = system[:, 0:BLOCK] + jnp.where(diagonal, RIDGE_WEIGHT, 0.0)
        for q in range(p + 1, blocks):
            matrix_ref[q * BLOCK:(q + 1) * BLOCK, low:low + BLOCK] = system[
                :, (q - p) * BLOCK:(q - p + 1) * BLOCK
            ].T
    eliminate(matrix_ref, 0, done)


def first_half(mine, arrived, slots_all, rows_total, done):
    size = slots_all.shape[1]
    return pl.pallas_call(
        functools.partial(first_half_kernel, rows_total=rows_total, done=done),
        out_shape=(
            jax.ShapeDtypeStruct((size, size), jnp.float32),
            jax.ShapeDtypeStruct((1, size), jnp.float32),
        ),
        in_specs=[VMEM, VMEM, HBM],
        out_specs=(VMEM, VMEM),
        scratch_shapes=[
            pltpu.VMEM((2, *slab_shape(size)), jnp.float32),
            pltpu.VMEM(slots_all.shape, jnp.float32),
            pltpu.SemaphoreType.DMA,
        ],
        compiler_params=PARAMS,
        cost_estimate=pl.CostEstimate(flops=12 * 10**9, bytes_accessed=2**20, transcendentals=0),
    )(mine, arrived, slots_all)


def second_half_kernel(matrix_ref, *refs, done):
    out_ref = refs[-1]
    blocks = matrix_ref.shape[0] // BLOCK
    out_ref[...] = matrix_ref[...]
    eliminate(out_ref, done, blocks)


def second_half(matrix, done, *after):
    return pl.pallas_call(
        functools.partial(second_half_kernel, done=done),
        out_shape=jax.ShapeDtypeStruct(matrix.shape, jnp.float32),
        in_specs=[VMEM] + [HBM] * len(after),
        out_specs=VMEM,
        input_output_aliases={0: 0},
        compiler_params=PARAMS,
        cost_estimate=pl.CostEstimate(flops=12 * 10**9, bytes_accessed=2**20, transcendentals=0),
    )(matrix, *after)


def solve_one_kernel(tensor_ref, total_ref, inverse_ref, weight_ref, *refs, items, slots, last):
    raw_ref, parts_ref, mine_ref, other_ref, out_ref, held_ref, pieces_ref, arrived, strips_ref = refs

    def ready():
        height = total_ref.shape[0] // (items * slots)
        count = items * slots
        blocks = [total_ref[n * height:(n + 1) * height, :] for z in range(slots) for n in range(z, count, slots)]
        raw = dot_full(jnp.concatenate(blocks, axis=0), inverse_ref[...])
        raw_ref[...] = raw
        store_gram(raw, strips_ref)
        mine_ref[...] = strips_ref[0]
        other_ref[...] = strips_ref[1]
        store_parts(raw, parts_ref)

    contraction_kernel(
        tensor_ref, parts_ref, weight_ref, out_ref, held_ref, pieces_ref, arrived,
        contract=0, first=0, last=last, ahead=None, load="first", ready=ready,
    )


def solve_one(tensor, total, inverse, weights, items, slots, last):
    depth, width = total.shape
    cols = tensor.shape[2]
    slab = jax.ShapeDtypeStruct(slab_shape(width), jnp.float32)
    out_shape = (
        jax.ShapeDtypeStruct(total.shape, jnp.float32),
        jax.ShapeDtypeStruct((3 * depth, width), jnp.bfloat16),
        slab,
        slab,
        jax.ShapeDtypeStruct((cols, width), jnp.float32),
        jax.ShapeDtypeStruct(tensor.shape, tensor.dtype),
    )
    return pl.pallas_call(
        functools.partial(solve_one_kernel, items=items, slots=slots, last=last),
        out_shape=out_shape,
        in_specs=[HBM, VMEM, VMEM, VMEM],
        out_specs=(VMEM,) * len(out_shape),
        scratch_shapes=[
            pltpu.VMEM((2 * cols, 2 * depth), jnp.bfloat16),
            pltpu.SemaphoreType.DMA((6,)),
            pltpu.VMEM((2, *slab_shape(width)), jnp.float32),
        ],
        compiler_params=PARAMS,
    )(tensor, total, inverse, weights)


def solve_two_kernel(total_ref, scale_ref, inverse_ref, raw_ref, squares_ref):
    raw = dot_full(total_ref[...] / scale_ref[...], inverse_ref[...])
    raw_ref[...] = raw
    squares_ref[...] = jnp.broadcast_to(jnp.sum(raw * raw, axis=0, keepdims=True), squares_ref.shape)


def solve_two(total, scale, inverse, copies):
    return pl.pallas_call(
        solve_two_kernel,
        out_shape=(
            jax.ShapeDtypeStruct(total.shape, jnp.float32),
            jax.ShapeDtypeStruct((copies, total.shape[1]), jnp.float32),
        ),
        in_specs=[VMEM, VMEM, VMEM],
        out_specs=(VMEM, VMEM),
        compiler_params=PARAMS,
    )(total, scale, inverse)


def exchange(values, axes):
    return lax.all_to_all(values, axes, 0, 0, tiled=True)


def sum_and_copy_kernel(received_ref, copies_ref, *, parts):
    height = received_ref.shape[0] // parts
    total = received_ref[0:height, :]
    for p in range(1, parts):
        total = total + received_ref[p * height:(p + 1) * height, :]
    for p in range(copies_ref.shape[0] // height):
        copies_ref[p * height:(p + 1) * height, :] = total


def sum_and_spread(received, parts, axes, copies):
    rows, cols = received.shape
    copied = pl.pallas_call(
        functools.partial(sum_and_copy_kernel, parts=parts),
        out_shape=jax.ShapeDtypeStruct((rows // parts * copies, cols), jnp.float32),
        in_specs=[VMEM],
        out_specs=VMEM,
        compiler_params=PARAMS,
    )(received)
    return exchange(copied, axes)


def swap(values, axis, mask):
    return lax.ppermute(values, axis, [(i, i ^ mask) for i in range(lax.axis_size(axis))])


def shift(values, axis, table):
    return lax.ppermute(values, axis, list(enumerate(table)))


def local(tensor, b_factor, c_factor):
    width = b_factor.shape[1]
    segs, items, slots = (lax.axis_size(name) for name in ("seg", "item", "slot"))
    depth = tensor.shape[0]

    def to_slot(value, d):
        return shift(value, "slot", [(i + d) % slots for i in range(slots)])

    def along_x(value, d):
        return shift(value, "item", [(i + 2 * d) % items for i in range(items)])

    *b_pieces, b_parts, one_ahead, held, c_rows = first_quarter(tensor, b_factor, c_factor, 1, items // 2)

    def part_one(held, c_rows, ahead, source=None):
        return contraction(held, b_parts, c_rows, 1, 0, depth, (), ahead, source)

    arrived = [along_x(b_pieces[d], d) for d in range(1, items // 2)]
    one_ahead = to_slot(one_ahead, 1)
    two_ahead, held = part_one(held, c_rows, 2, tensor)
    *arrived, one_ahead, two_ahead, c_rows = lax.optimization_barrier((*arrived, one_ahead, two_ahead, c_rows))
    piece = sum(arrived, b_pieces[0])
    other = swap(piece, "item", 1)
    two_ahead = to_slot(two_ahead, 2)
    three_ahead, held = part_one(held, c_rows, 3)
    other, three_ahead = lax.optimization_barrier((other, three_ahead))
    three_ahead = to_slot(three_ahead, 3)
    piece = piece + other
    pieces = [piece] + [along_x(piece, d) for d in range(1, items // 2)]
    two_ahead, c_rows = lax.optimization_barrier((two_ahead, c_rows))
    own, held = part_one(held, c_rows, 0)
    *pieces, own, three_ahead = lax.optimization_barrier((*pieces, own, three_ahead))
    pieces = jnp.stack(pieces)
    arrived = swap(pieces, "seg", 1)
    own, slots_all = finish_one(own, c_rows, (one_ahead, two_ahead, three_ahead))
    one_received = exchange(own, "item")

    matrix, ones = first_half(pieces, arrived, slots_all, None, 1)
    ones, one_received = lax.optimization_barrier((ones, one_received))
    one_total = sum_and_spread(one_received, items, ("item", "slot"), items * slots)
    inverse = second_half(matrix, 1, ones)
    segment_raw, a_parts, mine, other, two, held = solve_one(tensor, one_total, inverse, c_rows, items, slots, 4)

    arrived = swap(other, "seg", 1)
    two, held = contraction(held, a_parts, c_rows, 0, 4, 12, (two,), source=tensor)
    arrived, two = lax.optimization_barrier((arrived, two))
    mine = mine + arrived
    arrived = swap(mine, "seg", 2)
    two, held = contraction(held, a_parts, c_rows, 0, 12, depth, (two,))
    arrived, two = lax.optimization_barrier((arrived, two))
    mine = mine + arrived
    mine, two = lax.optimization_barrier((mine, two))
    arrived = swap(mine, "seg", 1)

    two_received = exchange(two, ("seg", "slot"))
    matrix, scale = first_half(mine, arrived, slots_all, tensor.shape[1] * segs, 2)
    scale, two_received = lax.optimization_barrier((scale, two_received))
    two_total = sum_and_spread(two_received, segs * slots, ("seg", "slot"), segs * slots)
    inverse = second_half(matrix, 2)
    a_factor = segment_raw / scale
    item_raw, squares = solve_two(two_total, scale, inverse, 8 * items)
    squares = jnp.sum(exchange(squares, "item").reshape(items, 8, width)[:, 0], axis=0)
    lambda_b = jnp.sqrt(squares / (tensor.shape[2] * items) + EPSILON)
    b_new = item_raw / lambda_b[None, :]
    return (a_factor, b_new, scale.reshape(width), lambda_b)


def solution(mesh):
    placed = (P("slot", "seg", "item"), P("item", None), P("slot", None))
    return jax.shard_map(
        local,
        mesh=mesh,
        in_specs=placed,
        out_specs=(P("seg", None), P("item", None), P(), P()),
        check_vma=False,
    )
```

```python
import functools

import jax
import jax.numpy as jnp
from jax import lax
from jax.experimental import pallas as pl
from jax.experimental.pallas import tpu as pltpu
from jax.sharding import PartitionSpec as P

RIDGE_WEIGHT = 0.1
EPSILON = 1e-06
HIGHEST = lax.Precision.HIGHEST
BLOCK = 128
PANEL = 16
GROUP = 4
VMEM = pl.BlockSpec(memory_space=pltpu.VMEM)
HBM = pl.BlockSpec(memory_space=pltpu.HBM)
PARAMS = pltpu.CompilerParams(vmem_limit_bytes=24 * 1024 * 1024)


def dot_full(left, right, left_dim=1):
    return lax.dot_general(
        left, right, (((left_dim,), (0,)), ((), ())), precision=HIGHEST, preferred_element_type=jnp.float32
    )


def dot_parts(left, right):
    return lax.dot_general(left, right, (((1,), (0,)), ((), ())), preferred_element_type=jnp.float32)


def split_two(values):
    high = values.astype(jnp.bfloat16)
    return high, (values - high.astype(jnp.float32)).astype(jnp.bfloat16)


def strip_place(strip):
    return ((0, 0), (1, 0), (1, 3 * BLOCK), (0, 4 * BLOCK))[strip]


def core_index():
    return lax.rem(lax.axis_index("seg"), 2)


def store_gram(rows, strips_ref):
    width = rows.shape[1]
    core = core_index()
    for strip in range(width // BLOCK):
        slab, start = strip_place(strip)
        low = strip * BLOCK
        place = core if slab == 0 else 1 - core
        strips_ref[place, :, start:start + width - low] = dot_full(rows[:, low:low + BLOCK], rows[:, low:], 0)


def store_parts(values, parts_ref):
    depth = values.shape[0]
    high, low = split_two(values)
    parts_ref[0:depth, :] = high
    parts_ref[depth:2 * depth, :] = high
    parts_ref[2 * depth:3 * depth, :] = low


def slab_shape(width):
    return (BLOCK, width + BLOCK)


def contraction_kernel(*refs, contract, first, last, ahead, load, ready=None):
    if load == "first":
        source_ref, parts_ref, weight_ref, *start_refs, out_ref, tensor_ref, pieces_ref, arrived = refs
        filled_ref = tensor_ref
    elif load == "rest":
        source_ref, parts_ref, weight_ref, *start_refs, tensor_ref, out_ref, filled_ref, pieces_ref, arrived = refs
    else:
        parts_ref, weight_ref, *start_refs, tensor_ref, out_ref, unused, pieces_ref = refs
    depth = parts_ref.shape[0] // 3
    cols = tensor_ref.shape[2]
    height = tensor_ref.shape[1]
    rows = pl.ds(0, height)
    if ahead is not None:
        slots = lax.axis_size("slot")
        height = height // slots

        def quarter(distance):
            return pl.ds(pl.multiple_of(lax.rem(lax.axis_index("slot") + distance, slots) * height, height), height)

        rows = quarter(ahead)
    group = GROUP if contract == 1 else 1
    half = pieces_ref.shape[0] // 2

    waiting = {}
    total_slots = tensor_ref.shape[0]
    if load == "first":
        if ahead is None:
            bounds = (first, first + 1, first + 3, last, last + 8)
            steps = [(rows, low, high) for low, high in zip(bounds, bounds[1:])]
        else:
            steps = [(rows, low, high) for low, high in ((0, 4), (4, 12), (12, total_slots))]
            steps += [(quarter(ahead + 1), 0, total_slots)]
    elif load == "rest":
        if ahead is None:
            steps = [(rows, last, total_slots)]
        else:
            steps = [(quarter(ahead + distance), 0, total_slots) for distance in range(1, slots - 1)]
    if load:
        for n, (place, low, high) in enumerate(steps):
            here = (pl.ds(low, high - low), place, slice(None))
            waiting[n] = pltpu.make_async_copy(source_ref.at[here], filled_ref.at[here], arrived.at[n])
            waiting[n].start()

    if ready is not None:
        ready()

    def prepare(k):
        for n in list(waiting):
            if load == "first" and steps[n][0] is rows and steps[n][1] == k:
                waiting.pop(n).wait()
        here = pl.ds(k // group % 2 * half, half)
        upper, lower = split_two(tensor_ref[k:k + group, rows, :].reshape(group * height, cols))
        pieces_ref[here, 0:depth] = upper if contract == 1 else upper.T
        pieces_ref[here, depth:2 * depth] = lower if contract == 1 else lower.T

    def product(k):
        here = pl.ds(k // group % 2 * half, half)
        return dot_parts(pieces_ref[here, :], parts_ref[0:2 * depth, :]) + dot_parts(
            pieces_ref[here, 0:depth], parts_ref[2 * depth:3 * depth, :]
        )

    size = half // group
    prepare(first)
    for k in range(first, last, group):
        if k + group < last:
            prepare(k + group)
        term = product(k)
        total = sum(term[n * size:(n + 1) * size, :] * weight_ref[k + n:k + n + 1, :] for n in range(group))
        if k == first:
            out_ref[0:size, :] = sum((ref[0:size, :] for ref in start_refs), total)
        else:
            out_ref[0:size, :] += total
    if out_ref.shape[0] > size:
        out_ref[size:, :] = weight_ref[...]
    for copy in waiting.values():
        copy.wait()


def contraction(held, parts, weights, contract, first, last, start=(), ahead=None, source=None):
    slots, rows, cols = held.shape
    width = parts.shape[1]
    height = rows if ahead is None else rows // lax.axis_size("slot")
    out_rows = height if contract == 1 else cols
    if ahead:
        out_rows += slots
    load = None if source is None else "rest"
    kernel = functools.partial(contraction_kernel, contract=contract, first=first, last=last, ahead=ahead, load=load)
    inputs = [parts, weights, *start, held]
    out_shape = jax.ShapeDtypeStruct((out_rows, width), jnp.float32)
    pieces = pltpu.VMEM((2 * (GROUP * height if contract == 1 else cols), 2 * parts.shape[0] // 3), jnp.bfloat16)
    sources = [source] if load else []
    return pl.pallas_call(
        kernel,
        in_specs=[HBM] * len(sources) + [VMEM] * len(inputs),
        out_specs=(VMEM, VMEM),
        out_shape=(out_shape, jax.ShapeDtypeStruct(held.shape, held.dtype)),
        scratch_shapes=[pieces] + ([pltpu.SemaphoreType.DMA((6,))] if load else []),
        input_output_aliases={len(sources) + len(inputs) - 1: 1},
        compiler_params=PARAMS,
        cost_estimate=pl.CostEstimate(flops=10**6, bytes_accessed=10**4, transcendentals=0),
    )(*sources, *inputs)


def first_quarter_kernel(tensor_ref, rows_ref, slots_ref, *refs, ahead):
    *piece_refs, parts_ref, out_ref, held_ref, weight_ref, pieces_ref, arrived, strips_ref, factor_ref, fetched = refs
    copies = (
        pltpu.make_async_copy(rows_ref, factor_ref, fetched.at[0]),
        pltpu.make_async_copy(slots_ref, weight_ref, fetched.at[1]),
    )
    for copy in copies:
        copy.start()

    def ready():
        copies[0].wait()
        rows = factor_ref[...]
        store_parts(rows, parts_ref)
        store_gram(rows, strips_ref)
        along = lax.axis_index("item") // 2
        height = piece_refs[0].shape[0]
        for distance, ref in enumerate(piece_refs):
            owner = lax.rem(along + distance, len(piece_refs))
            ref[...] = strips_ref[0, pl.ds(pl.multiple_of(owner * height, height), height), :]
        copies[1].wait()

    contraction_kernel(
        tensor_ref, parts_ref, weight_ref, out_ref, held_ref, pieces_ref, arrived,
        contract=1, first=0, last=tensor_ref.shape[0], ahead=ahead, load="first", ready=ready,
    )


def first_quarter(tensor, rows, slots, ahead, count):
    depth, width = rows.shape
    height = tensor.shape[1] // lax.axis_size("slot")
    piece = jax.ShapeDtypeStruct((BLOCK // count, width + BLOCK), jnp.float32)
    out_shape = (piece,) * count + (
        jax.ShapeDtypeStruct((3 * depth, width), jnp.bfloat16),
        jax.ShapeDtypeStruct((height + slots.shape[0], width), jnp.float32),
        jax.ShapeDtypeStruct(tensor.shape, tensor.dtype),
        jax.ShapeDtypeStruct(slots.shape, slots.dtype),
    )
    return pl.pallas_call(
        functools.partial(first_quarter_kernel, ahead=ahead),
        in_specs=[HBM, HBM, HBM],
        out_specs=(VMEM,) * len(out_shape),
        out_shape=out_shape,
        scratch_shapes=[
            pltpu.VMEM((2 * GROUP * height, 2 * depth), jnp.bfloat16),
            pltpu.SemaphoreType.DMA((6,)),
            pltpu.VMEM((2, *slab_shape(width)), jnp.float32),
            pltpu.VMEM(rows.shape, jnp.float32),
            pltpu.SemaphoreType.DMA((2,)),
        ],
        compiler_params=PARAMS,
    )(tensor, rows, slots)


def finish_one_kernel(own_ref, slots_ref, *refs):
    *arrived_refs, total_ref, slots_all_ref = refs
    height, depth = own_ref.shape[0], slots_ref.shape[0]
    total_ref[...] = sum((ref[0:height, :] for ref in arrived_refs), own_ref[...])
    slots_all_ref[0:depth, :] = slots_ref[...]
    for n, ref in enumerate(arrived_refs):
        slots_all_ref[(n + 1) * depth:(n + 2) * depth, :] = ref[height:, :]


def finish_one(own, slots, arrived):
    return pl.pallas_call(
        finish_one_kernel,
        out_shape=(
            jax.ShapeDtypeStruct(own.shape, jnp.float32),
            jax.ShapeDtypeStruct((slots.shape[0] * (1 + len(arrived)), slots.shape[1]), jnp.float32),
        ),
        in_specs=[VMEM] * (2 + len(arrived)),
        out_specs=(VMEM, VMEM),
        compiler_params=PARAMS,
    )(own, slots, *arrived)


def invert_block(block):
    size = block.shape[0]
    shape = (PANEL, size)
    sub = lax.broadcasted_iota(jnp.int32, shape, 0)
    lane = lax.broadcasted_iota(jnp.int32, shape, 1)
    row_index = lax.broadcasted_iota(jnp.int32, (size, size), 0)
    col_index = lax.broadcasted_iota(jnp.int32, (size, size), 1)
    panel = block[0:PANEL, :]
    for low in range(0, size, PANEL):
        high = low + PANEL
        columns = [jnp.broadcast_to(panel[:, low + t:low + t + 1], shape) for t in range(PANEL)]
        result = jnp.where((lane >= low) & (lane < high), jnp.where(lane - low == sub, 1.0, 0.0), panel)
        for t in range(PANEL):
            here = sub == t
            column = columns[t]
            scale = 1.0 / column[t:t + 1, :]
            for u in range(t + 1, PANEL):
                entry = columns[u][t:t + 1, :]
                pivot = entry * scale
                change = (column * entry) * scale if u == t + 1 else column * pivot
                columns[u] = jnp.where(here, jnp.broadcast_to(pivot, shape), columns[u] - change)
            pivot = result[t:t + 1, :] * scale
            result = jnp.where(here, jnp.broadcast_to(pivot, shape), result - column * pivot)
        if high < size:
            ahead = block[high:high + PANEL, :]
            panel = jnp.where((lane >= low) & (lane < high), 0.0, ahead)
            sums = [None] * 4
            for t in range(PANEL):
                term = jnp.broadcast_to(ahead[:, low + t:low + t + 1], shape) * result[t:t + 1, :]
                sums[t % 4] = term if sums[t % 4] is None else sums[t % 4] + term
            panel = panel - ((sums[0] + sums[1]) + (sums[2] + sums[3]))
        parts = [result]
        if low:
            parts.insert(0, jnp.zeros((low, size), jnp.float32))
        if high < size:
            parts.append(jnp.zeros((size - high, size), jnp.float32))
        padded = jnp.concatenate(parts, axis=0)
        update = dot_full(block, padded)
        kept = jnp.where((col_index >= low) & (col_index < high), 0.0, block)
        block = jnp.where((row_index >= low) & (row_index < high), padded, kept - update)
    return block


def eliminate(matrix_ref, first, last):
    size = matrix_ref.shape[0]

    def step(p, carry):
        low = pl.multiple_of(p * BLOCK, BLOCK)
        here = pl.ds(low, BLOCK)
        inverse = invert_block(matrix_ref[here, here])
        column = matrix_ref[:, here]
        matrix_ref[:, here] = jnp.zeros((size, BLOCK), jnp.float32)
        matrix_ref[here, here] = jnp.eye(BLOCK, dtype=jnp.float32)
        row = dot_full(inverse, matrix_ref[here, :])
        matrix_ref[...] = matrix_ref[...] - dot_full(column, row)
        matrix_ref[here, :] = row
        return carry

    lax.fori_loop(first, last, step, 0)


def place_rows(piece_refs, strips_ref):
    core = core_index()
    item = lax.axis_index("item")
    along = item // 2
    count, height, unused = piece_refs[0].shape
    for other_core, ref in enumerate(piece_refs):
        slab = core if other_core == 0 else 1 - core
        for back in range(count):
            owner = lax.rem(along + count - back, count)
            strips_ref[slab, pl.ds(pl.multiple_of(owner * height, height), height), :] = ref[back]


def place_slabs(piece_refs, strips_ref):
    core = core_index()
    strips_ref[core] = piece_refs[0][...]
    strips_ref[1 - core] = piece_refs[1][...]


def first_half_kernel(
    mine_ref, arrived_ref, source_ref, matrix_ref, scale_ref, strips_ref, slots_ref, copied, *, rows_total, done
):
    copy = pltpu.make_async_copy(source_ref, slots_ref, copied)
    copy.start()
    size = matrix_ref.shape[0]
    blocks = size // BLOCK
    diagonal = lax.broadcasted_iota(jnp.int32, (BLOCK, BLOCK), 0) == lax.broadcasted_iota(
        jnp.int32, (BLOCK, BLOCK), 1
    )
    if rows_total is None:
        place_rows((mine_ref, arrived_ref), strips_ref)
        scale_ref[...] = jnp.ones_like(scale_ref)
    else:
        place_slabs((mine_ref, arrived_ref), strips_ref)
        for p in range(blocks):
            slab, start = strip_place(p)
            squares = jnp.where(diagonal, strips_ref[slab, :, start:start + BLOCK], 0.0)
            scale_ref[:, p * BLOCK:(p + 1) * BLOCK] = jnp.sqrt(
                jnp.sum(squares, axis=0, keepdims=True) / rows_total + EPSILON
            )
    copy.wait()
    slots = slots_ref[...]
    for p in range(blocks):
        slab, start = strip_place(p)
        low = p * BLOCK
        gram = strips_ref[slab, :, start:start + size - low]
        if rows_total is not None:
            squares = jnp.where(diagonal, gram[:, 0:BLOCK], 0.0)
            scale = jnp.sqrt(jnp.sum(squares, axis=1, keepdims=True) / rows_total + EPSILON)
            gram = gram / scale / scale_ref[:, low:]
        system = gram * dot_full(slots[:, low:low + BLOCK], slots[:, low:], 0)
        matrix_ref[low:low + BLOCK, low:] = system
        matrix_ref[low:low + BLOCK, low:low + BLOCK] = system[:, 0:BLOCK] + jnp.where(diagonal, RIDGE_WEIGHT, 0.0)
        for q in range(p + 1, blocks):
            matrix_ref[q * BLOCK:(q + 1) * BLOCK, low:low + BLOCK] = system[
                :, (q - p) * BLOCK:(q - p + 1) * BLOCK
            ].T
    eliminate(matrix_ref, 0, done)


def first_half(mine, arrived, slots_all, rows_total, done):
    size = slots_all.shape[1]
    return pl.pallas_call(
        functools.partial(first_half_kernel, rows_total=rows_total, done=done),
        out_shape=(
            jax.ShapeDtypeStruct((size, size), jnp.float32),
            jax.ShapeDtypeStruct((1, size), jnp.float32),
        ),
        in_specs=[VMEM, VMEM, HBM],
        out_specs=(VMEM, VMEM),
        scratch_shapes=[
            pltpu.VMEM((2, *slab_shape(size)), jnp.float32),
            pltpu.VMEM(slots_all.shape, jnp.float32),
            pltpu.SemaphoreType.DMA,
        ],
        compiler_params=PARAMS,
        cost_estimate=pl.CostEstimate(flops=12 * 10**9, bytes_accessed=2**20, transcendentals=0),
    )(mine, arrived, slots_all)


def second_half_kernel(matrix_ref, *refs, done):
    out_ref = refs[-1]
    blocks = matrix_ref.shape[0] // BLOCK
    out_ref[...] = matrix_ref[...]
    eliminate(out_ref, done, blocks)


def second_half(matrix, done, *after):
    return pl.pallas_call(
        functools.partial(second_half_kernel, done=done),
        out_shape=jax.ShapeDtypeStruct(matrix.shape, jnp.float32),
        in_specs=[VMEM] + [HBM] * len(after),
        out_specs=VMEM,
        input_output_aliases={0: 0},
        compiler_params=PARAMS,
        cost_estimate=pl.CostEstimate(flops=12 * 10**9, bytes_accessed=2**20, transcendentals=0),
    )(matrix, *after)


def solve_one_kernel(tensor_ref, total_ref, inverse_ref, weight_ref, *refs, items, slots, last):
    raw_ref, parts_ref, mine_ref, other_ref, out_ref, held_ref, pieces_ref, arrived, strips_ref = refs

    def ready():
        height = total_ref.shape[0] // (items * slots)
        count = items * slots
        blocks = [total_ref[n * height:(n + 1) * height, :] for z in range(slots) for n in range(z, count, slots)]
        raw = dot_full(jnp.concatenate(blocks, axis=0), inverse_ref[...])
        raw_ref[...] = raw
        store_gram(raw, strips_ref)
        mine_ref[...] = strips_ref[0]
        other_ref[...] = strips_ref[1]
        store_parts(raw, parts_ref)

    contraction_kernel(
        tensor_ref, parts_ref, weight_ref, out_ref, held_ref, pieces_ref, arrived,
        contract=0, first=0, last=last, ahead=None, load="first", ready=ready,
    )


def solve_one(tensor, total, inverse, weights, items, slots, last):
    depth, width = total.shape
    cols = tensor.shape[2]
    slab = jax.ShapeDtypeStruct(slab_shape(width), jnp.float32)
    out_shape = (
        jax.ShapeDtypeStruct(total.shape, jnp.float32),
        jax.ShapeDtypeStruct((3 * depth, width), jnp.bfloat16),
        slab,
        slab,
        jax.ShapeDtypeStruct((cols, width), jnp.float32),
        jax.ShapeDtypeStruct(tensor.shape, tensor.dtype),
    )
    return pl.pallas_call(
        functools.partial(solve_one_kernel, items=items, slots=slots, last=last),
        out_shape=out_shape,
        in_specs=[HBM, VMEM, VMEM, VMEM],
        out_specs=(VMEM,) * len(out_shape),
        scratch_shapes=[
            pltpu.VMEM((2 * cols, 2 * depth), jnp.bfloat16),
            pltpu.SemaphoreType.DMA((6,)),
            pltpu.VMEM((2, *slab_shape(width)), jnp.float32),
        ],
        compiler_params=PARAMS,
    )(tensor, total, inverse, weights)


def solve_two_kernel(total_ref, scale_ref, inverse_ref, raw_ref, squares_ref):
    raw = dot_full(total_ref[...] / scale_ref[...], inverse_ref[...])
    raw_ref[...] = raw
    squares_ref[...] = jnp.broadcast_to(jnp.sum(raw * raw, axis=0, keepdims=True), squares_ref.shape)


def solve_two(total, scale, inverse, copies):
    return pl.pallas_call(
        solve_two_kernel,
        out_shape=(
            jax.ShapeDtypeStruct(total.shape, jnp.float32),
            jax.ShapeDtypeStruct((copies, total.shape[1]), jnp.float32),
        ),
        in_specs=[VMEM, VMEM, VMEM],
        out_specs=(VMEM, VMEM),
        compiler_params=PARAMS,
    )(total, scale, inverse)


def exchange(values, axes):
    return lax.all_to_all(values, axes, 0, 0, tiled=True)


def sum_and_copy_kernel(received_ref, copies_ref, *, parts):
    height = received_ref.shape[0] // parts
    total = received_ref[0:height, :]
    for p in range(1, parts):
        total = total + received_ref[p * height:(p + 1) * height, :]
    for p in range(copies_ref.shape[0] // height):
        copies_ref[p * height:(p + 1) * height, :] = total


def sum_and_spread(received, parts, axes, copies):
    rows, cols = received.shape
    copied = pl.pallas_call(
        functools.partial(sum_and_copy_kernel, parts=parts),
        out_shape=jax.ShapeDtypeStruct((rows // parts * copies, cols), jnp.float32),
        in_specs=[VMEM],
        out_specs=VMEM,
        compiler_params=PARAMS,
    )(received)
    return exchange(copied, axes)


def swap(values, axis, mask):
    return lax.ppermute(values, axis, [(i, i ^ mask) for i in range(lax.axis_size(axis))])


def shift(values, axis, table):
    return lax.ppermute(values, axis, list(enumerate(table)))


def local(tensor, b_factor, c_factor):
    width = b_factor.shape[1]
    segs, items, slots = (lax.axis_size(name) for name in ("seg", "item", "slot"))
    depth = tensor.shape[0]

    def to_slot(value, d):
        return shift(value, "slot", [(i + d) % slots for i in range(slots)])

    def along_x(value, d):
        return shift(value, "item", [(i + 2 * d) % items for i in range(items)])

    *b_pieces, b_parts, one_ahead, held, c_rows = first_quarter(tensor, b_factor, c_factor, 1, items // 2)

    def part_one(held, c_rows, ahead, source=None):
        return contraction(held, b_parts, c_rows, 1, 0, depth, (), ahead, source)

    arrived = [along_x(b_pieces[d], d) for d in range(1, items // 2)]
    one_ahead = to_slot(one_ahead, 1)
    two_ahead, held = part_one(held, c_rows, 2, tensor)
    *arrived, one_ahead, two_ahead, c_rows = lax.optimization_barrier((*arrived, one_ahead, two_ahead, c_rows))
    piece = sum(arrived, b_pieces[0])
    other = swap(piece, "item", 1)
    two_ahead = to_slot(two_ahead, 2)
    three_ahead, held = part_one(held, c_rows, 3)
    other, three_ahead = lax.optimization_barrier((other, three_ahead))
    three_ahead = to_slot(three_ahead, 3)
    piece = piece + other
    pieces = [piece] + [along_x(piece, d) for d in range(1, items // 2)]
    two_ahead, c_rows = lax.optimization_barrier((two_ahead, c_rows))
    own, held = part_one(held, c_rows, 0)
    *pieces, own, three_ahead = lax.optimization_barrier((*pieces, own, three_ahead))
    pieces = jnp.stack(pieces)
    arrived = swap(pieces, "seg", 1)
    own, slots_all = finish_one(own, c_rows, (one_ahead, two_ahead, three_ahead))
    one_received = exchange(own, "item")

    matrix, ones = first_half(pieces, arrived, slots_all, None, 1)
    ones, one_received = lax.optimization_barrier((ones, one_received))
    one_total = sum_and_spread(one_received, items, ("item", "slot"), items * slots)
    inverse = second_half(matrix, 1, ones)
    segment_raw, a_parts, mine, other, two, held = solve_one(tensor, one_total, inverse, c_rows, items, slots, 4)

    arrived = swap(other, "seg", 1)
    two, held = contraction(held, a_parts, c_rows, 0, 4, 12, (two,), source=tensor)
    arrived, two = lax.optimization_barrier((arrived, two))
    mine = mine + arrived
    arrived = swap(mine, "seg", 2)
    two, held = contraction(held, a_parts, c_rows, 0, 12, depth, (two,))
    arrived, two = lax.optimization_barrier((arrived, two))
    mine = mine + arrived
    mine, two = lax.optimization_barrier((mine, two))
    arrived = swap(mine, "seg", 1)

    two_received = exchange(two, ("seg", "slot"))
    matrix, scale = first_half(mine, arrived, slots_all, tensor.shape[1] * segs, 2)
    scale, two_received = lax.optimization_barrier((scale, two_received))
    two_total = sum_and_spread(two_received, segs * slots, ("seg", "slot"), segs * slots)
    inverse = second_half(matrix, 2)
    a_factor = segment_raw / scale
    item_raw, squares = solve_two(two_total, scale, inverse, 8 * items)
    squares = jnp.sum(exchange(squares, "item").reshape(items, 8, width)[:, 0], axis=0)
    lambda_b = jnp.sqrt(squares / (tensor.shape[2] * items) + EPSILON)
    b_new = item_raw / lambda_b[None, :]
    return (a_factor, b_new, scale.reshape(width), lambda_b)


def solution(mesh):
    placed = (P("slot", "seg", "item"), P("item", None), P("slot", None))
    return jax.shard_map(
        local,
        mesh=mesh,
        in_specs=placed,
        out_specs=(P("seg", None), P("item", None), P(), P()),
        check_vma=False,
    )
```
